256 devices in a mesh: seq: 64 (over z, x, core), head: 4 (over y).
Axes of the slice: x: 4, y: 4, z: 8, core: 2. Of those that a mesh axis runs over, the one named last changes fastest.
Arguments:
- queries: bfloat16 [8192, 4096], P(('seq', 'head')), may hold values from -6 to 6
- keys: bfloat16 [8192, 4096], P(('seq', 'head')), may hold values from -6 to 6
- values: bfloat16 [8192, 4096], P(('seq', 'head')), may hold values from -6 to 6
- grad_out: bfloat16 [8192, 4096], P(('seq', 'head')), may hold values from -6 to 6
- random_blocks: int32 [32, 128, 3], replicated, may hold values from 0 to 127, as said below
- global_blocks: int32 [2], replicated, may hold values from 0 to 127
Outputs:
- attended: bfloat16 [8192, 4096], P(('seq', 'head'))
- grad_queries: bfloat16 [8192, 4096], P(('seq', 'head'))
- grad_keys: bfloat16 [8192, 4096], P(('seq', 'head'))
- grad_values: bfloat16 [8192, 4096], P(('seq', 'head'))
The draws below stay inside these ranges and needn't reach their ends.
Inputs may be any that keep to these rules, and one draw needn't show every extreme that they name: `random_blocks`: for the heads of one index of head and the query blocks of one index of seq, at most 2 random entries lie in the blocks of any one index of seq, and in every such group some index of seq holds exactly 2.
All inputs are finite; a program needn't handle non-finite values.
Results may differ from the reference program's by a relative error of at most 0.034.
Values may be sent and summed in bfloat16 or wider, within the bound.
A program may use at most 128 MiB of HBM per device.

```python
import jax
import jax.numpy as jnp
from jax import lax

HEADS = 32
HEAD_DIM = 128
BLOCK = 64
RAND_BLOCKS = 3
GLOB_BLOCKS = 2
SEQ_LEN = 8192
BLOCKS = 128
QBLK_DEV = 2
SEQ_SHARDS = 64
HEADS_DEV = 8
REQUESTS = 48
SLOTS = 2


def draw_queries(key, part):
    shape = (SEQ_LEN, HEADS * HEAD_DIM)
    filled = jax.random.truncated_normal(jax.random.fold_in(key, 11), -6.0, 6.0, shape, jnp.float32)
    return filled.astype(jnp.bfloat16)


def draw_keys(key, part):
    shape = (SEQ_LEN, HEADS * HEAD_DIM)
    filled = jax.random.truncated_normal(jax.random.fold_in(key, 12), -6.0, 6.0, shape, jnp.float32)
    return filled.astype(jnp.bfloat16)


def draw_random_blocks(key, part):
    groups = HEADS // HEADS_DEV
    pool_size = SEQ_SHARDS * SLOTS

    def draw_group(group_id):
        group_key = jax.random.fold_in(jax.random.fold_in(key, 31), group_id)
        first, second, third, fourth = jax.random.split(group_key, 4)
        busiest = jax.random.randint(first, (), 0, SEQ_SHARDS)
        holder = jnp.arange(pool_size, dtype=jnp.int32) // SLOTS
        ranking = jax.random.permutation(second, pool_size).astype(jnp.int32)
        ranking = jnp.where(holder == busiest, -1 - jnp.arange(pool_size, dtype=jnp.int32), ranking)
        picked = holder[jnp.argsort(ranking)[:REQUESTS]]
        picked = picked[jax.random.permutation(third, REQUESTS)]
        offset = jax.random.randint(fourth, (REQUESTS,), 0, QBLK_DEV)
        return picked * QBLK_DEV + offset
    drawn = jax.vmap(draw_group)(jnp.arange(groups * SEQ_SHARDS, dtype=jnp.int32))
    drawn = drawn.reshape(groups, SEQ_SHARDS, HEADS_DEV, QBLK_DEV, RAND_BLOCKS).transpose(0, 2, 1, 3, 4)
    return drawn.reshape(HEADS, BLOCKS, RAND_BLOCKS).astype(jnp.int32)


def block_scale(key, extent, pieces, least, largest):
    def one(position, blocks):
        heights = jax.random.uniform(jax.random.fold_in(jax.random.fold_in(key, 6), position), (blocks,), jnp.float32, least / len(pieces), largest / len(pieces))
        return jnp.repeat(jnp.exp(heights), extent[position] // blocks).reshape((-1,) + (1,) * (len(extent) - position - 1))

    loudness = one(*pieces[0])
    for cut in pieces[1:]:
        loudness = loudness * one(*cut)
    return loudness


def scatter_about(rng, extent, width, reach, cuts=(), held_as=jnp.bfloat16):
    values = jax.random.normal(rng, extent, jnp.float32) * width
    if len(cuts) > 0:
        values = block_scale(rng, extent, cuts, -0.22, 0.18) * values
    return jnp.clip(values, min=-reach, max=reach).astype(held_as)


def setup_inputs(seed: int = 0) -> dict:
    seeds = jax.random.split(jax.random.key(seed), 7)
    return {
        "queries": draw_queries(jax.random.fold_in(seeds[6], 71), 0),
        "keys": draw_keys(jax.random.fold_in(seeds[6], 71), 0),
        "values": scatter_about(seeds[2], (SEQ_LEN, HEADS * HEAD_DIM), 1.0, 6.0, ((0, 256),)),
        "grad_out": scatter_about(seeds[3], (SEQ_LEN, HEADS * HEAD_DIM), 1.0, 6.0, ((0, 256),)),
        "random_blocks": draw_random_blocks(jax.random.fold_in(seeds[6], 71), 0),
        "global_blocks": jax.random.randint(seeds[5], (GLOB_BLOCKS,), 0, BLOCKS).astype(jnp.int32),
    }


def reference(queries, keys, values, grad_out, random_blocks, global_blocks):
    score_scale = HEAD_DIM ** -0.5
    block_index = jnp.arange(BLOCKS, dtype=jnp.int32)
    split_at = 3 + GLOB_BLOCKS

    def one_head(head_id):
        def head_slice(array):
            return lax.dynamic_slice_in_dim(array, head_id * HEAD_DIM, HEAD_DIM, 1).reshape(BLOCKS, BLOCK, HEAD_DIM)

        query_float = head_slice(queries).astype(jnp.float32)
        key_rows = head_slice(keys)
        value_rows = head_slice(values)
        incoming_gradient = head_slice(grad_out).astype(jnp.float32)
        rand_list = lax.dynamic_index_in_dim(random_blocks, head_id, 0, keepdims=False).astype(jnp.int32)
        window_list = jnp.stack([block_index - 1, block_index, block_index + 1], axis=1)
        glob_list = jnp.broadcast_to(global_blocks[None, :].astype(jnp.int32), (BLOCKS, GLOB_BLOCKS))
        key_index = jnp.concatenate([window_list, glob_list, rand_list], axis=1)
        key_valid = jnp.concatenate([jnp.stack([block_index >= 1, block_index >= 0, block_index + 1 < BLOCKS], axis=1), jnp.ones((BLOCKS, GLOB_BLOCKS + RAND_BLOCKS), bool)], axis=1)
        clipped = jnp.clip(key_index, 0, BLOCKS - 1)
        key_blocks_gathered = key_rows[clipped].astype(jnp.float32)
        value_blocks_gathered = value_rows[clipped].astype(jnp.float32)
        attention_logits = jnp.einsum("cmp,clqp->cmlq", query_float, key_blocks_gathered) * score_scale
        attention_logits = jnp.where(key_valid[:, None, :, None], attention_logits, -jnp.inf)
        row_max = jnp.max(attention_logits, axis=(2, 3), keepdims=True)
        exponent = jnp.exp(attention_logits - row_max)
        row_sum = jnp.sum(exponent, axis=(2, 3), keepdims=True)
        probability = exponent / row_sum
        attention_weight = lax.optimization_barrier(probability.astype(jnp.bfloat16)).astype(jnp.float32)
        attended = jnp.einsum("qczt,qzth->qch", attention_weight, value_blocks_gathered).astype(jnp.bfloat16)
        row_delta = jnp.sum(incoming_gradient * attended.astype(jnp.float32), axis=2)
        probability_gradient = jnp.einsum("cmp,clqp->cmlq", incoming_gradient, value_blocks_gathered)
        logit_gradient = probability * (probability_gradient - row_delta[:, :, None, None])
        logit_gradient = lax.optimization_barrier(logit_gradient.astype(jnp.bfloat16)).astype(jnp.float32)
        query_gradient = (score_scale * jnp.einsum("qczt,qzth->qch", logit_gradient, key_blocks_gathered)).astype(jnp.bfloat16)
        key_contribution = score_scale * jnp.einsum("okrt,okp->ortp", logit_gradient, query_float)
        value_contribution = jnp.einsum("okrt,okp->ortp", attention_weight, incoming_gradient)

        def rounded_tail(term):
            tail = lax.optimization_barrier(term[:, split_at:].astype(jnp.bfloat16)).astype(jnp.float32)
            joined = jnp.concatenate([term[:, :split_at], tail], axis=1)
            return jnp.where(key_valid[:, :, None, None], joined, 0.0)

        empty = jnp.zeros((BLOCKS, BLOCK, HEAD_DIM), jnp.float32)
        grad_key = empty.at[clipped].add(rounded_tail(key_contribution)).astype(jnp.bfloat16)
        grad_value = empty.at[clipped].add(rounded_tail(value_contribution)).astype(jnp.bfloat16)
        return attended, query_gradient, grad_key, grad_value

    results = lax.map(one_head, jnp.arange(HEADS, dtype=jnp.int32))

    def to_rows(stacked):
        return stacked.transpose(1, 2, 0, 3).reshape(BLOCKS * BLOCK, HEADS * HEAD_DIM)

    return (to_rows(results[0]), to_rows(results[1]), to_rows(results[2]), to_rows(results[3]))
```

```python
import functools
import jax
import jax.numpy as jnp
from jax import lax
from jax.experimental import pallas as pl
from jax.experimental.pallas import tpu as pltpu
from jax.sharding import PartitionSpec as P

HEAD_DIM = 128
BLOCK = 64
SCALE = HEAD_DIM ** -0.5
BLOCKS = 128
LOCAL = 16
NT = (((1,), (1,)), ((), ()))
TN = (((0,), (0,)), ((), ()))


def dot(a, b, dims=(((1,), (0,)), ((), ()))):
    return lax.dot_general(a, b, dims, preferred_element_type=jnp.float32)


def attention_kernel(rand_ref, glob_ref, place_ref, qg_ref, kv_ref, out_ref, dkv_ref, acc):
    acc[...] = jnp.zeros_like(acc)
    place = place_ref[0]

    def one(local, carry):
        block = (local // 2) * 16 + place * 2 + local % 2
        names = [
            jnp.maximum(block - 1, 0),
            block,
            jnp.minimum(block + 1, BLOCKS - 1),
            glob_ref[0],
            glob_ref[1],
        ] + [rand_ref[block * 3 + r] for r in range(3)]
        starts = [pl.multiple_of(n * BLOCK, BLOCK) for n in names]
        rows = pl.ds(pl.multiple_of(local * BLOCK, BLOCK), BLOCK)
        q = qg_ref[0, rows, :]
        g = qg_ref[1, rows, :]
        k = jnp.concatenate([kv_ref[0, pl.ds(s, BLOCK), :] for s in starts], axis=0)
        v = jnp.concatenate([kv_ref[1, pl.ds(s, BLOCK), :] for s in starts], axis=0)
        lane = lax.broadcasted_iota(jnp.int32, (1, 8 * BLOCK), 1) // BLOCK
        gone = ((lane == 0) & (block == 0)) | ((lane == 2) & (block == BLOCKS - 1))
        bias = jnp.where(gone, -jnp.inf, 0.0)
        s = dot(q, k, NT) * SCALE + bias
        dp = dot(g, v, NT)
        e = jnp.exp(s - jnp.max(s, axis=1, keepdims=True))
        p = e * (1.0 / jnp.sum(e, axis=1, keepdims=True))
        w = p.astype(jnp.bfloat16)
        o = dot(w, v).astype(jnp.bfloat16)
        delta = jnp.sum(g.astype(jnp.float32) * o.astype(jnp.float32), axis=1, keepdims=True)
        ds = (p * (dp - delta)).astype(jnp.bfloat16)
        out_ref[0, rows, :] = o
        out_ref[1, rows, :] = (SCALE * dot(ds, k)).astype(jnp.bfloat16)
        dk = dot(ds, q, TN)
        dv = dot(w, g, TN)
        for n, st in enumerate(starts):
            acc[0, pl.ds(st, BLOCK), :] += dk[n * BLOCK:(n + 1) * BLOCK]
            acc[1, pl.ds(st, BLOCK), :] += dv[n * BLOCK:(n + 1) * BLOCK]
        return carry

    lax.fori_loop(0, LOCAL, one, 0)

    def finish(t, carry):
        rows = pl.ds(pl.multiple_of(t * 256, 256), 256)
        dkv_ref[0, rows, :] = (SCALE * acc[0, rows, :]).astype(jnp.bfloat16)
        dkv_ref[1, rows, :] = acc[1, rows, :].astype(jnp.bfloat16)
        return carry

    lax.fori_loop(0, BLOCKS * BLOCK // 256, finish, 0)


def attention(rand, glob, place, qg, kv):
    vm = pl.BlockSpec(memory_space=pltpu.VMEM)
    sm = pl.BlockSpec(memory_space=pltpu.SMEM)
    return pl.pallas_call(
        attention_kernel,
        out_shape=(
            jax.ShapeDtypeStruct((2, LOCAL * BLOCK, HEAD_DIM), jnp.bfloat16),
            jax.ShapeDtypeStruct((2, BLOCKS * BLOCK, HEAD_DIM), jnp.bfloat16),
        ),
        in_specs=[sm, sm, sm, vm, vm],
        out_specs=(vm, vm),
        scratch_shapes=[pltpu.VMEM((2, BLOCKS * BLOCK, HEAD_DIM), jnp.float32)],
        compiler_params=pltpu.CompilerParams(vmem_limit_bytes=48 * 1024 * 1024),
    )(rand, glob, place, qg, kv)


def body(queries, keys, values, grad_out, random_blocks, global_blocks):
    z, x, c, y = (lax.axis_index(a) for a in ("z", "x", "core", "head"))
    rand = lax.dynamic_index_in_dim(random_blocks, z * 4 + y, 0, keepdims=False).reshape(-1)
    place = (x * 2 + c).reshape(1)
    stacked = jnp.stack([queries, grad_out, keys, values]).reshape(4, 32, 32, HEAD_DIM)
    got = lax.all_to_all(stacked, ("z", "head"), split_axis=2, concat_axis=1, tiled=False)
    qg = got[:2].reshape(2, LOCAL * BLOCK, HEAD_DIM)
    kv = lax.all_gather(got[2:], ("x", "core"), axis=0)
    kv = kv.reshape(8, 2, 8, 128, HEAD_DIM).transpose(1, 2, 0, 3, 4).reshape(2, BLOCKS * BLOCK, HEAD_DIM)
    out, dkv = attention(rand, global_blocks, place, qg, kv)
    dkv = dkv.reshape(2, 8, 8, 128, HEAD_DIM).transpose(2, 0, 1, 3, 4)
    dkv = lax.all_to_all(dkv, ("x", "core"), split_axis=0, concat_axis=0, tiled=True)
    dkv = jnp.sum(dkv.astype(jnp.float32), axis=0).astype(jnp.bfloat16)
    both = jnp.concatenate([out.reshape(2, 32, 32, HEAD_DIM), dkv.reshape(2, 32, 32, HEAD_DIM)])
    back = lax.all_to_all(both, ("z", "head"), split_axis=1, concat_axis=2, tiled=False)
    back = back.reshape(4, 32, 32 * HEAD_DIM)
    return back[0], back[1], back[2], back[3]


def solution(mesh):
    fine = jax.sharding.Mesh(mesh.devices.reshape(8, 4, 2, 4), ("z", "x", "core", "head"))
    rows = P(("z", "x", "core", "head"), None)
    return jax.shard_map(
        body,
        mesh=fine,
        in_specs=(rows, rows, rows, rows, P(), P()),
        out_specs=(rows, rows, rows, rows),
        check_vma=False,
    )
```

```python
import functools
import jax
import jax.numpy as jnp
from jax import lax
from jax.experimental import pallas as pl
from jax.experimental.pallas import tpu as pltpu
from jax.sharding import PartitionSpec as P

HEAD_DIM = 128
BLOCK = 64
SCALE = HEAD_DIM ** -0.5
BLOCKS = 128
LOCAL = 16
NT = (((1,), (1,)), ((), ()))
TN = (((0,), (0,)), ((), ()))


def dot(a, b, dims=(((1,), (0,)), ((), ()))):
    return lax.dot_general(a, b, dims, preferred_element_type=jnp.float32)


def attention_kernel(rand_ref, glob_ref, place_ref, qg_ref, kv_ref, out_ref, dkv_ref, acc):
    acc[...] = jnp.zeros_like(acc)
    place = place_ref[0]

    def one(local, carry):
        block = (local // 2) * 16 + place * 2 + local % 2
        names = [
            jnp.maximum(block - 1, 0),
            block,
            jnp.minimum(block + 1, BLOCKS - 1),
            glob_ref[0],
            glob_ref[1],
        ] + [rand_ref[block * 3 + r] for r in range(3)]
        starts = [pl.multiple_of(n * BLOCK, BLOCK) for n in names]
        rows = pl.ds(pl.multiple_of(local * BLOCK, BLOCK), BLOCK)
        q = qg_ref[0, rows, :]
        g = qg_ref[1, rows, :]
        k = jnp.concatenate([kv_ref[0, pl.ds(s, BLOCK), :] for s in starts], axis=0)
        v = jnp.concatenate([kv_ref[1, pl.ds(s, BLOCK), :] for s in starts], axis=0)
        lane = lax.broadcasted_iota(jnp.int32, (1, 8 * BLOCK), 1) // BLOCK
        gone = ((lane == 0) & (block == 0)) | ((lane == 2) & (block == BLOCKS - 1))
        bias = jnp.where(gone, -jnp.inf, 0.0)
        s = dot(q, k, NT) * SCALE + bias
        dp = dot(g, v, NT)
        e = jnp.exp(s - jnp.max(s, axis=1, keepdims=True))
        p = e * (1.0 / jnp.sum(e, axis=1, keepdims=True))
        w = p.astype(jnp.bfloat16)
        o = dot(w, v).astype(jnp.bfloat16)
        delta = jnp.sum(g.astype(jnp.float32) * o.astype(jnp.float32), axis=1, keepdims=True)
        ds = (p * (dp - delta)).astype(jnp.bfloat16)
        out_ref[0, rows, :] = o
        out_ref[1, rows, :] = (SCALE * dot(ds, k)).astype(jnp.bfloat16)
        dk = dot(ds, q, TN)
        dv = dot(w, g, TN)
        for n, st in enumerate(starts):
            acc[0, pl.ds(st, BLOCK), :] += dk[n * BLOCK:(n + 1) * BLOCK]
            acc[1, pl.ds(st, BLOCK), :] += dv[n * BLOCK:(n + 1) * BLOCK]
        return carry

    lax.fori_loop(0, LOCAL, one, 0)

    def finish(t, carry):
        rows = pl.ds(pl.multiple_of(t * 256, 256), 256)
        dkv_ref[0, rows, :] = (SCALE * acc[0, rows, :]).astype(jnp.bfloat16)
        dkv_ref[1, rows, :] = acc[1, rows, :].astype(jnp.bfloat16)
        return carry

    lax.fori_loop(0, BLOCKS * BLOCK // 256, finish, 0)


def attention(rand, glob, place, qg, kv):
    vm = pl.BlockSpec(memory_space=pltpu.VMEM)
    sm = pl.BlockSpec(memory_space=pltpu.SMEM)
    return pl.pallas_call(
        attention_kernel,
        out_shape=(
            jax.ShapeDtypeStruct((2, LOCAL * BLOCK, HEAD_DIM), jnp.bfloat16),
            jax.ShapeDtypeStruct((2, BLOCKS * BLOCK, HEAD_DIM), jnp.bfloat16),
        ),
        in_specs=[sm, sm, sm, vm, vm],
        out_specs=(vm, vm),
        scratch_shapes=[pltpu.VMEM((2, BLOCKS * BLOCK, HEAD_DIM), jnp.float32)],
        compiler_params=pltpu.CompilerParams(vmem_limit_bytes=48 * 1024 * 1024),
    )(rand, glob, place, qg, kv)

MESH = pl.DeviceIdType.MESH
NZ, NX, NC, NY = 8, 4, 2, 4
ROWS = 32
WIDTH = 4096
ORDER = (0, 1, 7, 2, 6, 3, 5, 4)


def places():
    return tuple(lax.axis_index(a) for a in ("z", "x", "core", "head"))


def greet(z, x, c, y):
    barrier = pltpu.get_barrier_semaphore()

    def hello(zz, xx, cc, yy):
        pl.semaphore_signal(barrier, inc=1, device_id=(zz, xx, cc, yy), device_id_type=MESH)

    hello(z, x, 1 - c, y)
    hello(z, (x + 1) % NX, c, y)
    hello(z, (x + 3) % NX, c, y)

    def one(i, carry):
        hello((z + i // NY) % NZ, x, c, (y + i % NY) % NY)
        return carry

    lax.fori_loop(1, NZ * NY, one, 0)
    pl.semaphore_wait(barrier, NZ * NY - 1 + 3)


def drain(like, sem):
    pltpu.make_async_copy(like, like, sem).wait()


def gather_kernel(q_ref, g_ref, k_ref, v_ref, qg_ref, kv_ref, stage, stage_sem, out_sem, ring_out_sem,
                  qg_sem, a_sem, l_sem, r_sem, f_sem, s_sem):
    z, x, c, y = places()
    loads = [
        pltpu.make_async_copy(src, stage.at[n], stage_sem.at[n])
        for n, src in ((2, k_ref), (3, v_ref), (0, q_ref), (1, g_ref))
    ]
    for load in loads:
        load.start()
    greet(z, x, c, y)
    right, left, over = (x + 1) % NX, (x + 3) % NX, (x + 2) % NX

    def columns(zz, yy):
        return pl.ds(pl.multiple_of((zz * NY + yy) * HEAD_DIM, HEAD_DIM), HEAD_DIM)

    mine = pl.ds(pl.multiple_of(y * ROWS, ROWS), ROWS)

    def scatter(step, first, dst, sem):
        zz = (z + ORDER[step]) % NZ

        def one(i, carry):
            yy = (y + i) % NY
            pltpu.make_async_remote_copy(
                src_ref=stage.at[pl.ds(first, 2), :, columns(zz, yy)], dst_ref=dst, send_sem=out_sem, recv_sem=sem,
                device_id=(zz, x, c, yy), device_id_type=MESH,
            ).start()
            return carry

        if ORDER[step] == 0:
            pltpu.make_async_copy(stage.at[pl.ds(first, 2), :, columns(z, y)], dst, sem).start()
        lax.fori_loop(1 if ORDER[step] == 0 else 0, NY, one, 0)

    loads[0].wait()
    loads[1].wait()
    for step in range(NZ):
        scatter(step, 2, kv_ref.at[:, z, x, c, mine, :], a_sem.at[z])
    loads[2].wait()
    loads[3].wait()

    def send(zz, xx, to, sem):
        part = kv_ref.at[:, zz, xx, c]
        pltpu.make_async_remote_copy(
            src_ref=part, dst_ref=part, send_sem=ring_out_sem, recv_sem=sem, device_id=to, device_id_type=MESH,
        ).start()

    to_right, to_left, to_twin = (z, right, c, y), (z, left, c, y), (z, x, 1 - c, y)
    source = [(z + NZ - d) % NZ for d in ORDER]
    for step in range(NZ + 2):
        if step < NZ:
            zz = source[step]
            drain(kv_ref.at[:, zz, x, c], a_sem.at[zz])
            send(zz, x, to_right, l_sem.at[zz])
            send(zz, x, to_left, r_sem.at[zz])
            send(zz, x, to_twin, s_sem)
            scatter(step, 0, qg_ref.at[:, z, mine, :], qg_sem)
        if 1 <= step < NZ + 1:
            zz = source[step - 1]
            drain(kv_ref.at[:, zz, left, c], l_sem.at[zz])
            if step % 2 == 0:
                send(zz, left, to_right, f_sem.at[zz])
            send(zz, left, to_twin, s_sem)
            drain(kv_ref.at[:, zz, right, c], r_sem.at[zz])
            if step % 2 == 1:
                send(zz, right, to_left, f_sem.at[zz])
            send(zz, right, to_twin, s_sem)
        if step >= 2:
            zz = source[step - 2]
            drain(kv_ref.at[:, zz, over, c], f_sem.at[zz])
            send(zz, over, to_twin, s_sem)
    drain(kv_ref.at[:, :, :, 1 - c], s_sem)
    drain(qg_ref, qg_sem)
    drain(stage.at[:, :, pl.ds(0, (NZ * NY - 1) * HEAD_DIM)], out_sem)
    drain(kv_ref.at[:, pl.ds(0, NZ - 1)], ring_out_sem)


def gather(q, g, k, v):
    hbm = pl.BlockSpec(memory_space=pl.ANY)
    dma = pltpu.SemaphoreType.DMA
    return pl.pallas_call(
        gather_kernel,
        out_shape=(
            jax.ShapeDtypeStruct((2, NZ, NY * ROWS, HEAD_DIM), jnp.bfloat16),
            jax.ShapeDtypeStruct((2, NZ, NX, NC, NY * ROWS, HEAD_DIM), jnp.bfloat16),
        ),
        in_specs=[hbm] * 4,
        out_specs=(hbm, hbm),
        scratch_shapes=[
            pltpu.VMEM((4, ROWS, WIDTH), jnp.bfloat16),
            dma((4,)), dma, dma, dma, dma((NZ,)), dma((NZ,)), dma((NZ,)), dma((NZ,)), dma,
        ],
        compiler_params=pltpu.CompilerParams(collective_id=0, has_side_effects=True),
    )(q, g, k, v)


def body(queries, keys, values, grad_out, random_blocks, global_blocks):
    z, x, c, y = places()
    rand = lax.dynamic_index_in_dim(random_blocks, z * NY + y, 0, keepdims=False).reshape(-1)
    place = (x * 2 + c).reshape(1)
    qg, kv = gather(queries, grad_out, keys, values)
    qg = qg.reshape(2, LOCAL * BLOCK, HEAD_DIM)
    kv = kv.reshape(2, BLOCKS * BLOCK, HEAD_DIM)
    out, dkv = attention(rand, global_blocks, place, qg, kv)
    dkv = dkv.reshape(2, 8, 8, 128, HEAD_DIM).transpose(2, 0, 1, 3, 4)
    dkv = lax.all_to_all(dkv, ("x", "core"), split_axis=0, concat_axis=0, tiled=True)
    dkv = jnp.sum(dkv.astype(jnp.float32), axis=0).astype(jnp.bfloat16)
    both = jnp.concatenate([out.reshape(2, 32, 32, HEAD_DIM), dkv.reshape(2, 32, 32, HEAD_DIM)])
    back = lax.all_to_all(both, ("z", "head"), split_axis=1, concat_axis=2, tiled=False)
    back = back.reshape(4, 32, 32 * HEAD_DIM)
    return back[0], back[1], back[2], back[3]


def solution(mesh):
    fine = jax.sharding.Mesh(mesh.devices.reshape(NZ, NX, NC, NY), ("z", "x", "core", "head"))
    rows = P(("z", "x", "core", "head"), None)
    return jax.shard_map(
        body,
        mesh=fine,
        in_specs=(rows, rows, rows, rows, P(), P()),
        out_specs=(rows, rows, rows, rows),
        check_vma=False,
    )
```

```python
import functools
import jax
import jax.numpy as jnp
from jax import lax
from jax.experimental import pallas as pl
from jax.experimental.pallas import tpu as pltpu
from jax.sharding import PartitionSpec as P

HEAD_DIM = 128
BLOCK = 64
SCALE = HEAD_DIM ** -0.5
BLOCKS = 128
LOCAL = 16
NT = (((1,), (1,)), ((), ()))
TN = (((0,), (0,)), ((), ()))


def dot(a, b, dims=(((1,), (0,)), ((), ()))):
    return lax.dot_general(a, b, dims, preferred_element_type=jnp.float32)


def attention_kernel(rand_ref, glob_ref, place_ref, qg_ref, kv_ref, out_ref, dkv_ref, acc):
    acc[...] = jnp.zeros_like(acc)
    place = place_ref[0]

    def one(local, carry):
        block = (local // 2) * 16 + place * 2 + local % 2
        names = [
            jnp.maximum(block - 1, 0),
            block,
            jnp.minimum(block + 1, BLOCKS - 1),
            glob_ref[0],
            glob_ref[1],
        ] + [rand_ref[block * 3 + r] for r in range(3)]
        starts = [pl.multiple_of(n * BLOCK, BLOCK) for n in names]
        rows = pl.ds(pl.multiple_of(local * BLOCK, BLOCK), BLOCK)
        q = qg_ref[0, rows, :]
        g = qg_ref[1, rows, :]
        k = jnp.concatenate([kv_ref[0, pl.ds(s, BLOCK), :] for s in starts], axis=0)
        v = jnp.concatenate([kv_ref[1, pl.ds(s, BLOCK), :] for s in starts], axis=0)
        lane = lax.broadcasted_iota(jnp.int32, (1, 8 * BLOCK), 1) // BLOCK
        gone = ((lane == 0) & (block == 0)) | ((lane == 2) & (block == BLOCKS - 1))
        bias = jnp.where(gone, -jnp.inf, 0.0)
        s = dot(q, k, NT) * SCALE + bias
        dp = dot(g, v, NT)
        e = jnp.exp(s - jnp.max(s, axis=1, keepdims=True))
        p = e * (1.0 / jnp.sum(e, axis=1, keepdims=True))
        w = p.astype(jnp.bfloat16)
        o = dot(w, v).astype(jnp.bfloat16)
        delta = jnp.sum(g.astype(jnp.float32) * o.astype(jnp.float32), axis=1, keepdims=True)
        ds = (p * (dp - delta)).astype(jnp.bfloat16)
        out_ref[0, rows, :] = o
        out_ref[1, rows, :] = (SCALE * dot(ds, k)).astype(jnp.bfloat16)
        dk = dot(ds, q, TN)
        dv = dot(w, g, TN)
        for n, st in enumerate(starts):
            acc[0, pl.ds(st, BLOCK), :] += dk[n * BLOCK:(n + 1) * BLOCK]
            acc[1, pl.ds(st, BLOCK), :] += dv[n * BLOCK:(n + 1) * BLOCK]
        return carry

    lax.fori_loop(0, LOCAL, one, 0)

    def finish(t, carry):
        rows = pl.ds(pl.multiple_of(t * 256, 256), 256)
        dkv_ref[0, rows, :] = (SCALE * acc[0, rows, :]).astype(jnp.bfloat16)
        dkv_ref[1, rows, :] = acc[1, rows, :].astype(jnp.bfloat16)
        return carry

    lax.fori_loop(0, BLOCKS * BLOCK // 256, finish, 0)


def attention(rand, glob, place, qg, kv):
    vm = pl.BlockSpec(memory_space=pltpu.VMEM)
    sm = pl.BlockSpec(memory_space=pltpu.SMEM)
    return pl.pallas_call(
        attention_kernel,
        out_shape=(
            jax.ShapeDtypeStruct((2, LOCAL * BLOCK, HEAD_DIM), jnp.bfloat16),
            jax.ShapeDtypeStruct((2, BLOCKS * BLOCK, HEAD_DIM), jnp.bfloat16),
        ),
        in_specs=[sm, sm, sm, vm, vm],
        out_specs=(vm, vm),
        scratch_shapes=[pltpu.VMEM((2, BLOCKS * BLOCK, HEAD_DIM), jnp.float32)],
        compiler_params=pltpu.CompilerParams(vmem_limit_bytes=48 * 1024 * 1024),
    )(rand, glob, place, qg, kv)

MESH = pl.DeviceIdType.MESH
NZ, NX, NC, NY = 8, 4, 2, 4
ROWS = 32
WIDTH = 4096
ORDER = (0, 1, 7, 2, 6, 3, 5, 4)


def places():
    return tuple(lax.axis_index(a) for a in ("z", "x", "core", "head"))


def greet(z, x, c, y):
    barrier = pltpu.get_barrier_semaphore()

    def hello(zz, xx, cc, yy):
        pl.semaphore_signal(barrier, inc=1, device_id=(zz, xx, cc, yy), device_id_type=MESH)

    hello(z, x, 1 - c, y)
    hello(z, (x + 1) % NX, c, y)
    hello(z, (x + 3) % NX, c, y)

    def one(i, carry):
        hello((z + i // NY) % NZ, x, c, (y + i % NY) % NY)
        return carry

    lax.fori_loop(1, NZ * NY, one, 0)
    pl.semaphore_wait(barrier, NZ * NY - 1 + 3)


def drain(like, sem):
    pltpu.make_async_copy(like, like, sem).wait()


def gather_kernel(q_ref, g_ref, k_ref, v_ref, qg_ref, kv_ref, stage, stage_sem, out_sem, ring_out_sem,
                  qg_sem, a_sem, l_sem, r_sem, f_sem, s_sem):
    z, x, c, y = places()
    loads = [
        pltpu.make_async_copy(src, stage.at[n], stage_sem.at[n])
        for n, src in ((2, k_ref), (3, v_ref), (0, q_ref), (1, g_ref))
    ]
    for load in loads:
        load.start()
    greet(z, x, c, y)
    right, left, over = (x + 1) % NX, (x + 3) % NX, (x + 2) % NX

    def columns(zz, yy):
        return pl.ds(pl.multiple_of((zz * NY + yy) * HEAD_DIM, HEAD_DIM), HEAD_DIM)

    mine = pl.ds(pl.multiple_of(y * ROWS, ROWS), ROWS)

    def scatter(step, first, dst, sem):
        zz = (z + ORDER[step]) % NZ

        def one(i, carry):
            yy = (y + i) % NY
            pltpu.make_async_remote_copy(
                src_ref=stage.at[pl.ds(first, 2), :, columns(zz, yy)], dst_ref=dst, send_sem=out_sem, recv_sem=sem,
                device_id=(zz, x, c, yy), device_id_type=MESH,
            ).start()
            return carry

        if ORDER[step] == 0:
            pltpu.make_async_copy(stage.at[pl.ds(first, 2), :, columns(z, y)], dst, sem).start()
        lax.fori_loop(1 if ORDER[step] == 0 else 0, NY, one, 0)

    loads[0].wait()
    loads[1].wait()
    for step in range(NZ):
        scatter(step, 2, kv_ref.at[:, z, x, c, mine, :], a_sem.at[z])
    loads[2].wait()
    loads[3].wait()

    def send(zz, xx, to, sem):
        part = kv_ref.at[:, zz, xx, c]
        pltpu.make_async_remote_copy(
            src_ref=part, dst_ref=part, send_sem=ring_out_sem, recv_sem=sem, device_id=to, device_id_type=MESH,
        ).start()

    to_right, to_left, to_twin = (z, right, c, y), (z, left, c, y), (z, x, 1 - c, y)
    source = [(z + NZ - d) % NZ for d in ORDER]
    for step in range(NZ + 2):
        if step < NZ:
            zz = source[step]
            drain(kv_ref.at[:, zz, x, c], a_sem.at[zz])
            send(zz, x, to_right, l_sem.at[zz])
            send(zz, x, to_left, r_sem.at[zz])
            send(zz, x, to_twin, s_sem)
            scatter(step, 0, qg_ref.at[:, z, mine, :], qg_sem)
        if 1 <= step < NZ + 1:
            zz = source[step - 1]
            drain(kv_ref.at[:, zz, left, c], l_sem.at[zz])
            if step % 2 == 0:
                send(zz, left, to_right, f_sem.at[zz])
            send(zz, left, to_twin, s_sem)
            drain(kv_ref.at[:, zz, right, c], r_sem.at[zz])
            if step % 2 == 1:
                send(zz, right, to_left, f_sem.at[zz])
            send(zz, right, to_twin, s_sem)
        if step >= 2:
            zz = source[step - 2]
            drain(kv_ref.at[:, zz, over, c], f_sem.at[zz])
            send(zz, over, to_twin, s_sem)
    drain(kv_ref.at[:, :, :, 1 - c], s_sem)
    drain(qg_ref, qg_sem)
    drain(stage.at[:, :, pl.ds(0, (NZ * NY - 1) * HEAD_DIM)], out_sem)
    drain(kv_ref.at[:, pl.ds(0, NZ - 1)], ring_out_sem)


def gather(q, g, k, v):
    hbm = pl.BlockSpec(memory_space=pl.ANY)
    dma = pltpu.SemaphoreType.DMA
    return pl.pallas_call(
        gather_kernel,
        out_shape=(
            jax.ShapeDtypeStruct((2, NZ, NY * ROWS, HEAD_DIM), jnp.bfloat16),
            jax.ShapeDtypeStruct((2, NZ, NX, NC, NY * ROWS, HEAD_DIM), jnp.bfloat16),
        ),
        in_specs=[hbm] * 4,
        out_specs=(hbm, hbm),
        scratch_shapes=[
            pltpu.VMEM((4, ROWS, WIDTH), jnp.bfloat16),
            dma((4,)), dma, dma, dma, dma((NZ,)), dma((NZ,)), dma((NZ,)), dma((NZ,)), dma,
        ],
        compiler_params=pltpu.CompilerParams(collective_id=0, has_side_effects=True),
    )(q, g, k, v)


BACK = (4, 3, 5, 2, 6, 1, 7, 0)


def return_kernel(od_ref, part_ref, od_out, kv_out, twin, sums, hop, joined, from_left, from_right, final,
                  twin_out, ring_out, od_send, kv_send, twin_sem, hop_sem, l_sem, r_sem, od_sem, kv_sem):
    z, x, c, y = places()
    greet(z, x, c, y)
    right, left, over = (x + 1) % NX, (x + 3) % NX, (x + 2) % NX
    planes = [(z + d) % NZ for d in BACK]
    columns = pl.ds(pl.multiple_of((z * NY + y) * HEAD_DIM, HEAD_DIM), HEAD_DIM)
    for step in range(NZ):
        pltpu.make_async_remote_copy(
            src_ref=part_ref.at[:, planes[step], :, 1 - c], dst_ref=twin.at[step], send_sem=twin_out,
            recv_sem=twin_sem.at[step], device_id=(z, x, 1 - c, y), device_id_type=MESH,
        ).start()

    def scatter(step, src, dst, send_sem, sem):
        def rows(yy):
            return src.at[:, pl.ds(pl.multiple_of(yy * ROWS, ROWS), ROWS), :]

        def one(i, carry):
            yy = (y + i) % NY
            pltpu.make_async_remote_copy(
                src_ref=rows(yy), dst_ref=dst.at[:, :, columns], send_sem=send_sem, recv_sem=sem,
                device_id=(planes[step], x, c, yy), device_id_type=MESH,
            ).start()
            return carry

        if BACK[step] == 0:
            pltpu.make_async_copy(rows(y), dst.at[:, :, columns], sem).start()
        lax.fori_loop(1 if BACK[step] == 0 else 0, NY, one, 0)

    for step in range(NZ):
        scatter(step, od_ref.at[:, planes[step]], od_out, od_send, od_sem)

    def pass_on(src, dst, sem, xx):
        pltpu.make_async_remote_copy(
            src_ref=src, dst_ref=dst, send_sem=ring_out, recv_sem=sem, device_id=(z, xx, c, y), device_id_type=MESH,
        ).start()

    def wide(a):
        return a.astype(jnp.float32)

    for step in range(NZ + 2):
        if step < NZ:
            drain(twin.at[step], twin_sem.at[step])

            def add(xx, carry, step=step):
                for n in range(2):
                    both = wide(part_ref[n, planes[step], xx, c]) + wide(twin[step, n, xx])
                    sums[step, n, xx] = both.astype(jnp.bfloat16)
                return carry

            lax.fori_loop(0, NX, add, 0)
            if step % 2 == 0:
                pass_on(sums.at[step, :, over], hop.at[step], hop_sem.at[step], right)
                pass_on(sums.at[step, :, left], from_right.at[step], r_sem.at[step], left)
            else:
                pass_on(sums.at[step, :, over], hop.at[step], hop_sem.at[step], left)
                pass_on(sums.at[step, :, right], from_left.at[step], l_sem.at[step], right)
        if 1 <= step < NZ + 1:
            k = step - 1
            drain(hop.at[k], hop_sem.at[k])
            to = right if k % 2 == 0 else left
            for n in range(2):
                joined[k, n] = (wide(sums[k, n, to]) + wide(hop[k, n])).astype(jnp.bfloat16)
            if k % 2 == 0:
                pass_on(joined.at[k], from_left.at[k], l_sem.at[k], right)
            else:
                pass_on(joined.at[k], from_right.at[k], r_sem.at[k], left)
        if step >= 2:
            k = step - 2
            drain(from_left.at[k], l_sem.at[k])
            drain(from_right.at[k], r_sem.at[k])
            for n in range(2):
                total = wide(sums[k, n, x]) + wide(from_left[k, n]) + wide(from_right[k, n])
                final[k, n] = total.astype(jnp.bfloat16)
            scatter(k, final.at[k], kv_out, kv_send, kv_sem)
    drain(part_ref.at[:, :, :, 0], twin_out)
    drain(sums.at[:, :, pl.ds(0, NX - 1)], ring_out)
    others = pl.ds(0, (NZ * NY - 1) * HEAD_DIM)
    drain(od_out.at[:, :, others], od_send)
    drain(kv_out.at[:, :, others], kv_send)
    drain(od_out, od_sem)
    drain(kv_out, kv_sem)


def give_back(od, part):
    hbm = pl.BlockSpec(memory_space=pl.ANY)
    vm = pl.BlockSpec(memory_space=pltpu.VMEM)
    dma = pltpu.SemaphoreType.DMA
    rows = jax.ShapeDtypeStruct((2, ROWS, WIDTH), jnp.bfloat16)
    chunk = pltpu.VMEM((NZ, 2, NY * ROWS, HEAD_DIM), jnp.bfloat16)
    wide_chunk = pltpu.VMEM((NZ, 2, NX, NY * ROWS, HEAD_DIM), jnp.bfloat16)
    each = dma((NZ,))
    return pl.pallas_call(
        return_kernel,
        out_shape=(rows, rows),
        in_specs=[vm, vm],
        out_specs=(hbm, hbm),
        scratch_shapes=[wide_chunk, wide_chunk] + [chunk] * 5 + [dma] * 4 + [each] * 4 + [dma, dma],
        compiler_params=pltpu.CompilerParams(
            collective_id=1, has_side_effects=True, vmem_limit_bytes=48 * 1024 * 1024
        ),
    )(od, part)


def body(queries, keys, values, grad_out, random_blocks, global_blocks):
    z, x, c, y = places()
    rand = lax.dynamic_index_in_dim(random_blocks, z * NY + y, 0, keepdims=False).reshape(-1)
    place = (x * 2 + c).reshape(1)
    qg, kv = gather(queries, grad_out, keys, values)
    qg = qg.reshape(2, LOCAL * BLOCK, HEAD_DIM)
    kv = kv.reshape(2, BLOCKS * BLOCK, HEAD_DIM)
    od, part = attention(rand, global_blocks, place, qg, kv)
    od, dkv = give_back(
        od.reshape(2, NZ, NY * ROWS, HEAD_DIM), part.reshape(2, NZ, NX, NC, NY * ROWS, HEAD_DIM)
    )
    return od[0], od[1], dkv[0], dkv[1]


def solution(mesh):
    fine = jax.sharding.Mesh(mesh.devices.reshape(NZ, NX, NC, NY), ("z", "x", "core", "head"))
    rows = P(("z", "x", "core", "head"), None)
    return jax.shard_map(
        body,
        mesh=fine,
        in_specs=(rows, rows, rows, rows, P(), P()),
        out_specs=(rows, rows, rows, rows),
        check_vma=False,
    )
```

```python
import functools
import jax
import jax.numpy as jnp
from jax import lax
from jax.experimental import pallas as pl
from jax.experimental.pallas import tpu as pltpu
from jax.sharding import PartitionSpec as P

HEAD_DIM = 128
BLOCK = 64
SCALE = HEAD_DIM ** -0.5
BLOCKS = 128
LOCAL = 16
NT = (((1,), (1,)), ((), ()))
TN = (((0,), (0,)), ((), ()))
GROUP = 8
NZ, NX, NC, NY = 8, 4, 2, 4


def places():
    return tuple(lax.axis_index(a) for a in ("z", "x", "core", "head"))


def dot(a, b, dims=(((1,), (0,)), ((), ()))):
    return lax.dot_general(a, b, dims, preferred_element_type=jnp.float32)


def attention_kernel(rand_hbm, glob_hbm, qg_ref, kv_ref, out_ref, dkv_ref, acc, rand_ref, glob_ref, sems):
    tables = [
        pltpu.make_async_copy(rand_hbm, rand_ref, sems.at[0]),
        pltpu.make_async_copy(glob_hbm, glob_ref, sems.at[1]),
    ]
    for table in tables:
        table.start()
    z, x, c, y = places()
    head = z * NY + y
    place = x * NC + c

    def clear(t, carry):
        rows = pl.ds(pl.multiple_of(t * 512, 512), 512)
        for n in range(2):
            acc[n, rows, :] = jnp.zeros((512, HEAD_DIM), jnp.float32)
        return carry

    lax.fori_loop(0, BLOCKS * BLOCK // 512, clear, 0)
    for table in tables:
        table.wait()
    lane = lax.broadcasted_iota(jnp.int32, (1, 8 * BLOCK), 1) // BLOCK

    def starts_of(block):
        names = [
            jnp.maximum(block - 1, 0),
            block,
            jnp.minimum(block + 1, BLOCKS - 1),
            glob_ref[0],
            glob_ref[1],
        ] + [rand_ref[r, head, block] for r in range(3)]
        return [pl.multiple_of(n * BLOCK, BLOCK) for n in names]

    def many(turn, carry):
        locals_ = [turn * GROUP + n for n in range(GROUP)]
        blocks = [(t // 2) * 16 + place * 2 + t % 2 for t in locals_]
        starts = [starts_of(b) for b in blocks]
        rows = [pl.ds(pl.multiple_of(t * BLOCK, BLOCK), BLOCK) for t in locals_]
        R = range(GROUP)
        q = [qg_ref[0, rows[n], :] for n in R]
        g = [qg_ref[1, rows[n], :] for n in R]
        k = [jnp.concatenate([kv_ref[0, pl.ds(s, BLOCK), :] for s in starts[n]], axis=0) for n in R]
        v = [jnp.concatenate([kv_ref[1, pl.ds(s, BLOCK), :] for s in starts[n]], axis=0) for n in R]
        s = [dot(q[n], k[n], NT) for n in R]
        dp = [dot(g[n], v[n], NT) for n in R]
        w, p, o, ds = [], [], [], []
        for n in R:
            gone = ((lane == 0) & (blocks[n] == 0)) | ((lane == 2) & (blocks[n] == BLOCKS - 1))
            t = s[n] * SCALE + jnp.where(gone, -jnp.inf, 0.0)
            e = jnp.exp(t - jnp.max(t, axis=1, keepdims=True))
            p.append(e * (1.0 / jnp.sum(e, axis=1, keepdims=True)))
            w.append(p[n].astype(jnp.bfloat16))
        for n in R:
            o.append(dot(w[n], v[n]).astype(jnp.bfloat16))
        dv = [dot(w[n], g[n], TN) for n in R]
        for n in R:
            delta = jnp.sum(g[n].astype(jnp.float32) * o[n].astype(jnp.float32), axis=1, keepdims=True)
            ds.append((p[n] * (dp[n] - delta)).astype(jnp.bfloat16))
        dq = [dot(ds[n], k[n]) for n in R]
        dk = [dot(ds[n], q[n], TN) for n in R]
        for n in R:
            out_ref[0, rows[n], :] = o[n]
            out_ref[1, rows[n], :] = (SCALE * dq[n]).astype(jnp.bfloat16)
            for i, st in enumerate(starts[n]):
                part = slice(i * BLOCK, (i + 1) * BLOCK)
                acc[0, pl.ds(st, BLOCK), :] += dk[n][part]
                acc[1, pl.ds(st, BLOCK), :] += dv[n][part]
        return carry

    lax.fori_loop(0, LOCAL // GROUP, many, 0)

    def finish(t, carry):
        rows = pl.ds(pl.multiple_of(t * 256, 256), 256)
        dkv_ref[0, rows, :] = (SCALE * acc[0, rows, :]).astype(jnp.bfloat16)
        dkv_ref[1, rows, :] = acc[1, rows, :].astype(jnp.bfloat16)
        return carry

    lax.fori_loop(0, BLOCKS * BLOCK // 256, finish, 0)


def attention(rand, glob, qg, kv):
    vm = pl.BlockSpec(memory_space=pltpu.VMEM)
    hbm = pl.BlockSpec(memory_space=pltpu.HBM)
    return pl.pallas_call(
        attention_kernel,
        out_shape=(
            jax.ShapeDtypeStruct((2, LOCAL * BLOCK, HEAD_DIM), jnp.bfloat16),
            jax.ShapeDtypeStruct((2, BLOCKS * BLOCK, HEAD_DIM), jnp.bfloat16),
        ),
        in_specs=[hbm, hbm, vm, vm],
        out_specs=(vm, vm),
        scratch_shapes=[
            pltpu.VMEM((2, BLOCKS * BLOCK, HEAD_DIM), jnp.float32),
            pltpu.SMEM(rand.shape, jnp.int32),
            pltpu.SMEM(glob.shape, jnp.int32),
            pltpu.SemaphoreType.DMA((2,)),
        ],
        compiler_params=pltpu.CompilerParams(vmem_limit_bytes=20 * 1024 * 1024),
    )(rand, glob, qg, kv)

MESH = pl.DeviceIdType.MESH
ROWS = 32
WIDTH = 4096
LAG1, LAG2 = 4, 8
ORDER = (0, 1, 7, 2, 6, 3, 5, 4)


def greet(z, x, c, y, zs, ys):
    barrier = pltpu.get_barrier_semaphore()

    def hello(zz, xx, cc, yy):
        pl.semaphore_signal(barrier, inc=1, device_id=(zz, xx, cc, yy), device_id_type=MESH)

    hello(z, x, 1 - c, y)
    hello(z, (x + 1) % NX, c, y)
    hello(z, (x + 3) % NX, c, y)

    for n in range(1, NZ * NY):
        hello(zs[n // NY], x, c, ys[n % NY])
    pl.semaphore_wait(barrier, NZ * NY - 1 + 3)


def drain(like, sem):
    pltpu.make_async_copy(like, like, sem).wait()


def gather_kernel(q_ref, g_ref, k_ref, v_ref, qg_ref, kv_ref, stage, stage_sem, out_sem, ring_out_sem,
                  qg_sem, a_sem, l_sem, r_sem, f_sem, s_sem):
    z, x, c, y = places()
    loads = [
        pltpu.make_async_copy(src, stage.at[n], stage_sem.at[n])
        for n, src in ((2, k_ref), (3, v_ref), (0, q_ref), (1, g_ref))
    ]
    for load in loads:
        load.start()
    zs = [(z + d) % NZ for d in range(NZ)]
    ys = [(y + d) % NY for d in range(NY)]
    greet(z, x, c, y, zs, ys)
    right, left, over = (x + 1) % NX, (x + 3) % NX, (x + 2) % NX

    def columns(zz, yy):
        return pl.ds(pl.multiple_of((zz * NY + yy) * HEAD_DIM, HEAD_DIM), HEAD_DIM)

    mine = pl.ds(pl.multiple_of(y * ROWS, ROWS), ROWS)

    def scatter(step, first, dst, sem):
        d = ORDER[step]
        for n in range(NY):
            part = stage.at[pl.ds(first, 2), :, columns(zs[d], ys[n])]
            if d == 0 and n == 0:
                pltpu.make_async_copy(part, dst, sem).start()
            else:
                pltpu.make_async_remote_copy(
                    src_ref=part, dst_ref=dst, send_sem=out_sem, recv_sem=sem,
                    device_id=(zs[d], x, c, ys[n]), device_id_type=MESH,
                ).start()

    loads[0].wait()
    loads[1].wait()
    for step in range(NZ):
        scatter(step, 2, kv_ref.at[:, z, x, c, mine, :], a_sem.at[z])
    loads[2].wait()
    loads[3].wait()

    def send(zz, xx, to, sem):
        part = kv_ref.at[:, zz, xx, c]
        pltpu.make_async_remote_copy(
            src_ref=part, dst_ref=part, send_sem=ring_out_sem, recv_sem=sem, device_id=to, device_id_type=MESH,
        ).start()

    to_right, to_left, to_twin = (z, right, c, y), (z, left, c, y), (z, x, 1 - c, y)
    source = [zs[(NZ - d) % NZ] for d in ORDER]
    for step in range(NZ + LAG2):
        if step < NZ:
            zz = source[step]
            drain(kv_ref.at[:, zz, x, c], a_sem.at[zz])
            send(zz, x, to_right, l_sem.at[zz])
            send(zz, x, to_left, r_sem.at[zz])
            send(zz, x, to_twin, s_sem)
            scatter(step, 0, qg_ref.at[:, z, mine, :], qg_sem)
        if LAG1 <= step < NZ + LAG1:
            k = step - LAG1
            zz = source[k]
            drain(kv_ref.at[:, zz, left, c], l_sem.at[zz])
            if k % 2 == 1:
                send(zz, left, to_right, f_sem.at[zz])
            send(zz, left, to_twin, s_sem)
            drain(kv_ref.at[:, zz, right, c], r_sem.at[zz])
            if k % 2 == 0:
                send(zz, right, to_left, f_sem.at[zz])
            send(zz, right, to_twin, s_sem)
        if step >= LAG2:
            zz = source[step - LAG2]
            drain(kv_ref.at[:, zz, over, c], f_sem.at[zz])
            send(zz, over, to_twin, s_sem)
    drain(kv_ref.at[:, :, :, 1 - c], s_sem)
    drain(qg_ref, qg_sem)
    drain(stage.at[:, :, pl.ds(0, (NZ * NY - 1) * HEAD_DIM)], out_sem)
    drain(kv_ref.at[:, pl.ds(0, NZ - 1)], ring_out_sem)


def gather(q, g, k, v):
    anywhere = pl.BlockSpec(memory_space=pl.ANY)
    dma = pltpu.SemaphoreType.DMA
    return pl.pallas_call(
        gather_kernel,
        out_shape=(
            jax.ShapeDtypeStruct((2, NZ, NY * ROWS, HEAD_DIM), jnp.bfloat16),
            jax.ShapeDtypeStruct((2, NZ, NX, NC, NY * ROWS, HEAD_DIM), jnp.bfloat16),
        ),
        in_specs=[pl.BlockSpec(memory_space=pltpu.HBM)] * 4,
        out_specs=(anywhere, anywhere),
        scratch_shapes=[
            pltpu.VMEM((4, ROWS, WIDTH), jnp.bfloat16),
            dma((4,)), dma, dma, dma, dma((NZ,)), dma((NZ,)), dma((NZ,)), dma((NZ,)), dma,
        ],
        compiler_params=pltpu.CompilerParams(
            collective_id=0, has_side_effects=True, vmem_limit_bytes=4 * 1024 * 1024
        ),
    )(q, g, k, v)


BACK1, BACK2 = 3, 6
BACK = (4, 3, 5, 2, 6, 1, 7, 0)


def return_kernel(od_ref, part_ref, od_out, kv_out, twin, sums, hop, joined, from_left, from_right, final,
                  twin_out, ring_out, od_send, kv_send, twin_sem, hop_sem, l_sem, r_sem, od_sem, kv_sem):
    z, x, c, y = places()
    zs = [(z + d) % NZ for d in range(NZ)]
    ys = [(y + d) % NY for d in range(NY)]
    greet(z, x, c, y, zs, ys)
    right, left, over = (x + 1) % NX, (x + 3) % NX, (x + 2) % NX
    planes = [zs[d] for d in BACK]
    columns = pl.ds(pl.multiple_of((z * NY + y) * HEAD_DIM, HEAD_DIM), HEAD_DIM)
    for step in range(NZ):
        pltpu.make_async_remote_copy(
            src_ref=part_ref.at[:, planes[step], :, 1 - c], dst_ref=twin.at[step], send_sem=twin_out,
            recv_sem=twin_sem.at[step], device_id=(z, x, 1 - c, y), device_id_type=MESH,
        ).start()

    def scatter(step, src, dst, send_sem, sem):
        def rows(yy):
            return src.at[:, pl.ds(pl.multiple_of(yy * ROWS, ROWS), ROWS), :]

        for n in range(NY):
            if BACK[step] == 0 and n == 0:
                pltpu.make_async_copy(rows(y), dst.at[:, :, columns], sem).start()
            else:
                pltpu.make_async_remote_copy(
                    src_ref=rows(ys[n]), dst_ref=dst.at[:, :, columns], send_sem=send_sem, recv_sem=sem,
                    device_id=(planes[step], x, c, ys[n]), device_id_type=MESH,
                ).start()

    for step in range(NZ):
        scatter(step, od_ref.at[:, planes[step]], od_out, od_send, od_sem)

    def pass_on(src, dst, sem, xx):
        pltpu.make_async_remote_copy(
            src_ref=src, dst_ref=dst, send_sem=ring_out, recv_sem=sem, device_id=(z, xx, c, y), device_id_type=MESH,
        ).start()

    def wide(a):
        return a.astype(jnp.float32)

    for step in range(NZ + BACK2):
        if step < NZ:
            drain(twin.at[step], twin_sem.at[step])

            def add(xx, carry, step=step):
                for n in range(2):
                    both = wide(part_ref[n, planes[step], xx, c]) + wide(twin[step, n, xx])
                    sums[step, n, xx] = both.astype(jnp.bfloat16)
                return carry

            lax.fori_loop(0, NX, add, 0)
            if step % 2 == 0:
                pass_on(sums.at[step, :, over], hop.at[step], hop_sem.at[step], right)
                pass_on(sums.at[step, :, left], from_right.at[step], r_sem.at[step], left)
            else:
                pass_on(sums.at[step, :, over], hop.at[step], hop_sem.at[step], left)
                pass_on(sums.at[step, :, right], from_left.at[step], l_sem.at[step], right)
        if BACK1 <= step < NZ + BACK1:
            k = step - BACK1
            drain(hop.at[k], hop_sem.at[k])
            to = right if k % 2 == 0 else left
            for n in range(2):
                joined[k, n] = (wide(sums[k, n, to]) + wide(hop[k, n])).astype(jnp.bfloat16)
            if k % 2 == 0:
                pass_on(joined.at[k], from_left.at[k], l_sem.at[k], right)
            else:
                pass_on(joined.at[k], from_right.at[k], r_sem.at[k], left)
        if step >= BACK2:
            k = step - BACK2
            drain(from_left.at[k], l_sem.at[k])
            drain(from_right.at[k], r_sem.at[k])
            for n in range(2):
                total = wide(sums[k, n, x]) + wide(from_left[k, n]) + wide(from_right[k, n])
                final[k, n] = total.astype(jnp.bfloat16)
            scatter(k, final.at[k], kv_out, kv_send, kv_sem)
    drain(part_ref.at[:, :, :, 0], twin_out)
    drain(sums.at[:, :, pl.ds(0, NX - 1)], ring_out)
    others = pl.ds(0, (NZ * NY - 1) * HEAD_DIM)
    drain(od_out.at[:, :, others], od_send)
    drain(kv_out.at[:, :, others], kv_send)
    drain(od_out, od_sem)
    drain(kv_out, kv_sem)


def give_back(od, part):
    hbm = pl.BlockSpec(memory_space=pl.ANY)
    vm = pl.BlockSpec(memory_space=pltpu.VMEM)
    dma = pltpu.SemaphoreType.DMA
    rows = jax.ShapeDtypeStruct((2, ROWS, WIDTH), jnp.bfloat16)
    chunk = pltpu.VMEM((NZ, 2, NY * ROWS, HEAD_DIM), jnp.bfloat16)
    wide_chunk = pltpu.VMEM((NZ, 2, NX, NY * ROWS, HEAD_DIM), jnp.bfloat16)
    each = dma((NZ,))
    return pl.pallas_call(
        return_kernel,
        out_shape=(rows, rows),
        in_specs=[vm, vm],
        out_specs=(hbm, hbm),
        scratch_shapes=[wide_chunk, wide_chunk] + [chunk] * 5 + [dma] * 4 + [each] * 4 + [dma, dma],
        compiler_params=pltpu.CompilerParams(
            collective_id=1, has_side_effects=True, vmem_limit_bytes=20 * 1024 * 1024
        ),
    )(od, part)


def body(queries, keys, values, grad_out, random_blocks, global_blocks):
    rand = jnp.transpose(random_blocks, (2, 0, 1))
    qg, kv = gather(queries, grad_out, keys, values)
    qg = qg.reshape(2, LOCAL * BLOCK, HEAD_DIM)
    kv = kv.reshape(2, BLOCKS * BLOCK, HEAD_DIM)
    od, part = attention(rand, global_blocks, qg, kv)
    od, dkv = give_back(
        od.reshape(2, NZ, NY * ROWS, HEAD_DIM), part.reshape(2, NZ, NX, NC, NY * ROWS, HEAD_DIM)
    )
    return od[0], od[1], dkv[0], dkv[1]


def solution(mesh):
    fine = jax.sharding.Mesh(mesh.devices.reshape(NZ, NX, NC, NY), ("z", "x", "core", "head"))
    rows = P(("z", "x", "core", "head"), None)
    return jax.shard_map(
        body,
        mesh=fine,
        in_specs=(rows, rows, rows, rows, P(), P()),
        out_specs=(rows, rows, rows, rows),
        check_vma=False,
    )
```

```python
import functools
import jax
import jax.numpy as jnp
from jax import lax
from jax.experimental import pallas as pl
from jax.experimental.pallas import tpu as pltpu
from jax.sharding import PartitionSpec as P

HEAD_DIM = 128
BLOCK = 64
SCALE = HEAD_DIM ** -0.5
BLOCKS = 128
LOCAL = 16
NT = (((1,), (1,)), ((), ()))
TN = (((0,), (0,)), ((), ()))
GROUP = 8
NZ, NX, NC, NY = 8, 4, 2, 4


def places():
    return tuple(lax.axis_index(a) for a in ("z", "x", "core", "head"))


def dot(a, b, dims=(((1,), (0,)), ((), ()))):
    return lax.dot_general(a, b, dims, preferred_element_type=jnp.float32)


def attention_kernel(rand_hbm, glob_hbm, qg_ref, kv_ref, out_ref, dkv_ref, acc, rand_ref, glob_ref, sems):
    tables = [
        pltpu.make_async_copy(rand_hbm, rand_ref, sems.at[0]),
        pltpu.make_async_copy(glob_hbm, glob_ref, sems.at[1]),
    ]
    for table in tables:
        table.start()
    z, x, c, y = places()
    head = z * NY + y
    place = x * NC + c

    def clear(t, carry):
        rows = pl.ds(pl.multiple_of(t * 512, 512), 512)
        for n in range(2):
            acc[n, rows, :] = jnp.zeros((512, HEAD_DIM), jnp.float32)
        return carry

    lax.fori_loop(0, BLOCKS * BLOCK // 512, clear, 0)
    for table in tables:
        table.wait()
    lane = lax.broadcasted_iota(jnp.int32, (1, 8 * BLOCK), 1) // BLOCK

    def starts_of(block):
        names = [
            jnp.maximum(block - 1, 0),
            block,
            jnp.minimum(block + 1, BLOCKS - 1),
            glob_ref[0],
            glob_ref[1],
        ] + [rand_ref[r, head, block] for r in range(3)]
        return [pl.multiple_of(n * BLOCK, BLOCK) for n in names]

    def many(turn, carry):
        locals_ = [turn * GROUP + n for n in range(GROUP)]
        blocks = [(t // 2) * 16 + place * 2 + t % 2 for t in locals_]
        starts = [starts_of(b) for b in blocks]
        rows = [pl.ds(pl.multiple_of(t * BLOCK, BLOCK), BLOCK) for t in locals_]
        R = range(GROUP)
        q = [qg_ref[0, rows[n], :] for n in R]
        g = [qg_ref[1, rows[n], :] for n in R]
        k = [jnp.concatenate([kv_ref[0, pl.ds(s, BLOCK), :] for s in starts[n]], axis=0) for n in R]
        v = [jnp.concatenate([kv_ref[1, pl.ds(s, BLOCK), :] for s in starts[n]], axis=0) for n in R]
        s = [dot(q[n], k[n], NT) for n in R]
        dp = [dot(g[n], v[n], NT) for n in R]
        w, p, o, ds = [], [], [], []
        for n in R:
            gone = ((lane == 0) & (blocks[n] == 0)) | ((lane == 2) & (blocks[n] == BLOCKS - 1))
            t = s[n] * SCALE + jnp.where(gone, -jnp.inf, 0.0)
            e = jnp.exp(t - jnp.max(t, axis=1, keepdims=True))
            p.append(e * (1.0 / jnp.sum(e, axis=1, keepdims=True)))
            w.append(p[n].astype(jnp.bfloat16))
        for n in R:
            o.append(dot(w[n], v[n]).astype(jnp.bfloat16))
        dv = [dot(w[n], g[n], TN) for n in R]
        for n in R:
            delta = jnp.sum(g[n].astype(jnp.float32) * o[n].astype(jnp.float32), axis=1, keepdims=True)
            ds.append((p[n] * (dp[n] - delta)).astype(jnp.bfloat16))
        dq = [dot(ds[n], k[n]) for n in R]
        dk = [dot(ds[n], q[n], TN) for n in R]
        for n in R:
            out_ref[0, rows[n], :] = o[n]
            out_ref[1, rows[n], :] = (SCALE * dq[n]).astype(jnp.bfloat16)
            for i, st in enumerate(starts[n]):
                part = slice(i * BLOCK, (i + 1) * BLOCK)
                acc[0, pl.ds(st, BLOCK), :] += dk[n][part]
                acc[1, pl.ds(st, BLOCK), :] += dv[n][part]
        return carry

    lax.fori_loop(0, LOCAL // GROUP, many, 0)

    def finish(t, carry):
        rows = pl.ds(pl.multiple_of(t * 256, 256), 256)
        dkv_ref[0, rows, :] = (SCALE * acc[0, rows, :]).astype(jnp.bfloat16)
        dkv_ref[1, rows, :] = acc[1, rows, :].astype(jnp.bfloat16)
        return carry

    lax.fori_loop(0, BLOCKS * BLOCK // 256, finish, 0)


def attention(rand, glob, qg, kv):
    vm = pl.BlockSpec(memory_space=pltpu.VMEM)
    hbm = pl.BlockSpec(memory_space=pltpu.HBM)
    return pl.pallas_call(
        attention_kernel,
        out_shape=(
            jax.ShapeDtypeStruct((2, LOCAL * BLOCK, HEAD_DIM), jnp.bfloat16),
            jax.ShapeDtypeStruct((2, BLOCKS * BLOCK, HEAD_DIM), jnp.bfloat16),
        ),
        in_specs=[hbm, hbm, vm, vm],
        out_specs=(vm, vm),
        scratch_shapes=[
            pltpu.VMEM((2, BLOCKS * BLOCK, HEAD_DIM), jnp.float32),
            pltpu.SMEM(rand.shape, jnp.int32),
            pltpu.SMEM(glob.shape, jnp.int32),
            pltpu.SemaphoreType.DMA((2,)),
        ],
        compiler_params=pltpu.CompilerParams(vmem_limit_bytes=20 * 1024 * 1024),
    )(*(pltpu.with_memory_space_constraint(a, pltpu.HBM) for a in (rand, glob)), qg, kv)

MESH = pl.DeviceIdType.MESH
ROWS = 32
WIDTH = 4096
LAG1, LAG2 = 4, 8
ORDER = (0, 1, 7, 2, 6, 3, 5, 4)


def greet(z, x, c, y, zs, ys):
    barrier = pltpu.get_barrier_semaphore()

    def hello(zz, xx, cc, yy):
        pl.semaphore_signal(barrier, inc=1, device_id=(zz, xx, cc, yy), device_id_type=MESH)

    hello(z, x, 1 - c, y)
    hello(z, (x + 1) % NX, c, y)
    hello(z, (x + 3) % NX, c, y)

    for n in range(1, NZ * NY):
        hello(zs[n // NY], x, c, ys[n % NY])
    pl.semaphore_wait(barrier, NZ * NY - 1 + 3)


def drain(like, sem):
    pltpu.make_async_copy(like, like, sem).wait()


def gather_kernel(q_ref, g_ref, k_ref, v_ref, qg_ref, kv_ref, stage, stage_sem, out_sem, ring_out_sem,
                  qg_sem, a_sem, l_sem, r_sem, f_sem, s_sem):
    z, x, c, y = places()
    loads = [
        pltpu.make_async_copy(src, stage.at[n], stage_sem.at[n])
        for n, src in ((2, k_ref), (3, v_ref), (0, q_ref), (1, g_ref))
    ]
    for load in loads:
        load.start()
    zs = [(z + d) % NZ for d in range(NZ)]
    ys = [(y + d) % NY for d in range(NY)]
    greet(z, x, c, y, zs, ys)
    right, left, over = (x + 1) % NX, (x + 3) % NX, (x + 2) % NX

    def columns(zz, yy):
        return pl.ds(pl.multiple_of((zz * NY + yy) * HEAD_DIM, HEAD_DIM), HEAD_DIM)

    mine = pl.ds(pl.multiple_of(y * ROWS, ROWS), ROWS)

    def scatter(step, first, dst, sem):
        d = ORDER[step]
        for n in range(NY):
            part = stage.at[pl.ds(first, 2), :, columns(zs[d], ys[n])]
            if d == 0 and n == 0:
                pltpu.make_async_copy(part, dst, sem).start()
            else:
                pltpu.make_async_remote_copy(
                    src_ref=part, dst_ref=dst, send_sem=out_sem, recv_sem=sem,
                    device_id=(zs[d], x, c, ys[n]), device_id_type=MESH,
                ).start()

    loads[0].wait()
    loads[1].wait()
    for step in range(NZ):
        scatter(step, 2, kv_ref.at[:, z, x, c, mine, :], a_sem.at[z])
    loads[2].wait()
    loads[3].wait()

    def send(zz, xx, to, sem):
        part = kv_ref.at[:, zz, xx, c]
        pltpu.make_async_remote_copy(
            src_ref=part, dst_ref=part, send_sem=ring_out_sem, recv_sem=sem, device_id=to, device_id_type=MESH,
        ).start()

    to_right, to_left, to_twin = (z, right, c, y), (z, left, c, y), (z, x, 1 - c, y)
    source = [zs[(NZ - d) % NZ] for d in ORDER]
    for step in range(NZ + LAG2):
        if step < NZ:
            zz = source[step]
            drain(kv_ref.at[:, zz, x, c], a_sem.at[zz])
            send(zz, x, to_right, l_sem.at[zz])
            send(zz, x, to_left, r_sem.at[zz])
            send(zz, x, to_twin, s_sem)
            scatter(step, 0, qg_ref.at[:, z, mine, :], qg_sem)
        if LAG1 <= step < NZ + LAG1:
            k = step - LAG1
            zz = source[k]
            drain(kv_ref.at[:, zz, left, c], l_sem.at[zz])
            if k % 2 == 1:
                send(zz, left, to_right, f_sem.at[zz])
            send(zz, left, to_twin, s_sem)
            drain(kv_ref.at[:, zz, right, c], r_sem.at[zz])
            if k % 2 == 0:
                send(zz, right, to_left, f_sem.at[zz])
            send(zz, right, to_twin, s_sem)
        if step >= LAG2:
            zz = source[step - LAG2]
            drain(kv_ref.at[:, zz, over, c], f_sem.at[zz])
            send(zz, over, to_twin, s_sem)
    drain(kv_ref.at[:, :, :, 1 - c], s_sem)
    drain(qg_ref, qg_sem)
    drain(stage.at[:, :, pl.ds(0, (NZ * NY - 1) * HEAD_DIM)], out_sem)
    drain(kv_ref.at[:, pl.ds(0, NZ - 1)], ring_out_sem)


def gather(q, g, k, v):
    anywhere = pl.BlockSpec(memory_space=pl.ANY)
    dma = pltpu.SemaphoreType.DMA
    return pl.pallas_call(
        gather_kernel,
        out_shape=(
            jax.ShapeDtypeStruct((2, NZ, NY * ROWS, HEAD_DIM), jnp.bfloat16),
            jax.ShapeDtypeStruct((2, NZ, NX, NC, NY * ROWS, HEAD_DIM), jnp.bfloat16),
        ),
        in_specs=[pl.BlockSpec(memory_space=pltpu.HBM)] * 4,
        out_specs=(anywhere, anywhere),
        scratch_shapes=[
            pltpu.VMEM((4, ROWS, WIDTH), jnp.bfloat16),
            dma((4,)), dma, dma, dma, dma((NZ,)), dma((NZ,)), dma((NZ,)), dma((NZ,)), dma,
        ],
        compiler_params=pltpu.CompilerParams(
            collective_id=0, has_side_effects=True, vmem_limit_bytes=4 * 1024 * 1024
        ),
    )(*(pltpu.with_memory_space_constraint(a, pltpu.HBM) for a in (q, g, k, v)))


BACK1, BACK2 = 2, 4
BACK = (4, 3, 5, 2, 6, 1, 7, 0)


def return_kernel(od_ref, part_ref, od_out, kv_out, twin, sums, hop, joined, from_left, from_right, final,
                  twin_out, ring_out, od_send, kv_send, twin_sem, hop_sem, l_sem, r_sem, od_sem, kv_sem):
    z, x, c, y = places()
    zs = [(z + d) % NZ for d in range(NZ)]
    ys = [(y + d) % NY for d in range(NY)]
    greet(z, x, c, y, zs, ys)
    right, left, over = (x + 1) % NX, (x + 3) % NX, (x + 2) % NX
    planes = [zs[d] for d in BACK]
    columns = pl.ds(pl.multiple_of((z * NY + y) * HEAD_DIM, HEAD_DIM), HEAD_DIM)
    for step in range(NZ):
        pltpu.make_async_remote_copy(
            src_ref=part_ref.at[:, planes[step], :, 1 - c], dst_ref=twin.at[step], send_sem=twin_out,
            recv_sem=twin_sem.at[step], device_id=(z, x, 1 - c, y), device_id_type=MESH,
        ).start()

    def scatter(step, src, dst, send_sem, sem):
        def rows(yy):
            return src.at[:, pl.ds(pl.multiple_of(yy * ROWS, ROWS), ROWS), :]

        for n in range(NY):
            if BACK[step] == 0 and n == 0:
                pltpu.make_async_copy(rows(y), dst.at[:, :, columns], sem).start()
            else:
                pltpu.make_async_remote_copy(
                    src_ref=rows(ys[n]), dst_ref=dst.at[:, :, columns], send_sem=send_sem, recv_sem=sem,
                    device_id=(planes[step], x, c, ys[n]), device_id_type=MESH,
                ).start()

    for step in range(NZ):
        scatter(step, od_ref.at[:, planes[step]], od_out, od_send, od_sem)

    def pass_on(src, dst, sem, xx):
        pltpu.make_async_remote_copy(
            src_ref=src, dst_ref=dst, send_sem=ring_out, recv_sem=sem, device_id=(z, xx, c, y), device_id_type=MESH,
        ).start()

    def wide(a):
        return a.astype(jnp.float32)

    for step in range(NZ + BACK2):
        if step < NZ:
            drain(twin.at[step], twin_sem.at[step])

            def add(xx, carry, step=step):
                for n in range(2):
                    both = wide(part_ref[n, planes[step], xx, c]) + wide(twin[step, n, xx])
                    sums[step, n, xx] = both.astype(jnp.bfloat16)
                return carry

            lax.fori_loop(0, NX, add, 0)
            if step % 2 == 0:
                pass_on(sums.at[step, :, over], hop.at[step], hop_sem.at[step], right)
                pass_on(sums.at[step, :, left], from_right.at[step], r_sem.at[step], left)
            else:
                pass_on(sums.at[step, :, over], hop.at[step], hop_sem.at[step], left)
                pass_on(sums.at[step, :, right], from_left.at[step], l_sem.at[step], right)
        if BACK1 <= step < NZ + BACK1:
            k = step - BACK1
            drain(hop.at[k], hop_sem.at[k])
            to = right if k % 2 == 0 else left
            for n in range(2):
                joined[k, n] = (wide(sums[k, n, to]) + wide(hop[k, n])).astype(jnp.bfloat16)
            if k % 2 == 0:
                pass_on(joined.at[k], from_left.at[k], l_sem.at[k], right)
            else:
                pass_on(joined.at[k], from_right.at[k], r_sem.at[k], left)
        if step >= BACK2:
            k = step - BACK2
            drain(from_left.at[k], l_sem.at[k])
            drain(from_right.at[k], r_sem.at[k])
            for n in range(2):
                total = wide(sums[k, n, x]) + wide(from_left[k, n]) + wide(from_right[k, n])
                final[k, n] = total.astype(jnp.bfloat16)
            scatter(k, final.at[k], kv_out, kv_send, kv_sem)
    drain(part_ref.at[:, :, :, 0], twin_out)
    drain(sums.at[:, :, pl.ds(0, NX - 1)], ring_out)
    others = pl.ds(0, (NZ * NY - 1) * HEAD_DIM)
    drain(od_out.at[:, :, others], od_send)
    drain(kv_out.at[:, :, others], kv_send)
    drain(od_out, od_sem)
    drain(kv_out, kv_sem)


def give_back(od, part):
    hbm = pl.BlockSpec(memory_space=pl.ANY)
    vm = pl.BlockSpec(memory_space=pltpu.VMEM)
    dma = pltpu.SemaphoreType.DMA
    rows = jax.ShapeDtypeStruct((2, ROWS, WIDTH), jnp.bfloat16)
    chunk = pltpu.VMEM((NZ, 2, NY * ROWS, HEAD_DIM), jnp.bfloat16)
    wide_chunk = pltpu.VMEM((NZ, 2, NX, NY * ROWS, HEAD_DIM), jnp.bfloat16)
    each = dma((NZ,))
    return pl.pallas_call(
        return_kernel,
        out_shape=(rows, rows),
        in_specs=[vm, vm],
        out_specs=(hbm, hbm),
        scratch_shapes=[wide_chunk, wide_chunk] + [chunk] * 5 + [dma] * 4 + [each] * 4 + [dma, dma],
        compiler_params=pltpu.CompilerParams(
            collective_id=1, has_side_effects=True, vmem_limit_bytes=20 * 1024 * 1024
        ),
    )(od, part)


def body(queries, keys, values, grad_out, random_blocks, global_blocks):
    rand = jnp.transpose(random_blocks, (2, 0, 1))
    qg, kv = gather(queries, grad_out, keys, values)
    qg = qg.reshape(2, LOCAL * BLOCK, HEAD_DIM)
    kv = kv.reshape(2, BLOCKS * BLOCK, HEAD_DIM)
    od, part = attention(rand, global_blocks, qg, kv)
    od, dkv = give_back(
        od.reshape(2, NZ, NY * ROWS, HEAD_DIM), part.reshape(2, NZ, NX, NC, NY * ROWS, HEAD_DIM)
    )
    return od[0], od[1], dkv[0], dkv[1]


def solution(mesh):
    fine = jax.sharding.Mesh(mesh.devices.reshape(NZ, NX, NC, NY), ("z", "x", "core", "head"))
    rows = P(("z", "x", "core", "head"), None)
    return jax.shard_map(
        body,
        mesh=fine,
        in_specs=(rows, rows, rows, rows, P(), P()),
        out_specs=(rows, rows, rows, rows),
        check_vma=False,
    )
```

```python
import functools
import jax
import jax.numpy as jnp
from jax import lax
from jax.experimental import pallas as pl
from jax.experimental.pallas import tpu as pltpu
from jax.sharding import PartitionSpec as P

HEAD_DIM = 128
BLOCK = 64
SCALE = HEAD_DIM ** -0.5
BLOCKS = 128
MESH = pl.DeviceIdType.MESH
NZ, NX, NC, NY = 8, 4, 2, 4
ROWS = 32
WIDTH = 4096
ORDER = (0, 1, 7, 2, 6, 3, 5, 4)
BACK = (4, 3, 5, 2, 6, 1, 7, 0)
QORDER = (4, 3, 5, 2, 6, 1, 7, 0)
LAG1, LAG2 = 4, 8
BACK1, BACK2 = 2, 4
TURN = 4
NEAR = 4
RANDS = 3
WINDOW_TERMS = NZ * NEAR
TERMS = WINDOW_TERMS + NZ * 2 * RANDS + 2
FAR = 1000
NT = (((1,), (1,)), ((), ()))
TN = (((0,), (0,)), ((), ()))


def dot(a, b, dims=(((1,), (0,)), ((), ()))):
    return lax.dot_general(a, b, dims, preferred_element_type=jnp.float32)


def wide(a):
    return a.astype(jnp.float32)


def narrow(a):
    return a.astype(jnp.bfloat16)


def places():
    return tuple(lax.axis_index(a) for a in ("z", "x", "core", "head"))


def greet(z, x, c, y, zs, ys):
    barrier = pltpu.get_barrier_semaphore()

    def hello(zz, xx, cc, yy):
        pl.semaphore_signal(barrier, inc=1, device_id=(zz, xx, cc, yy), device_id_type=MESH)

    hello(z, x, 1 - c, y)
    hello(z, (x + 1) % NX, c, y)
    hello(z, (x + 3) % NX, c, y)
    for n in range(1, NZ * NY):
        hello(zs[n // NY], x, c, ys[n % NY])
    pl.semaphore_wait(barrier, NZ * NY - 1 + 3)


def drain(like, sem):
    pltpu.make_async_copy(like, like, sem).wait()


def columns(zz, yy):
    return pl.ds(pl.multiple_of((zz * NY + yy) * HEAD_DIM, HEAD_DIM), HEAD_DIM)


def quarter(yy):
    return pl.ds(pl.multiple_of(yy * ROWS, ROWS), ROWS)


def layer_kernel(rand_hbm, glob_hbm, q_ref, g_ref, k_ref, v_ref, od_out, dkv_out,
                 stage, kv, qg, od, terms, total, table, twin_send, twin, sums, hop, joined, from_left, from_right, final,
                 rand, glob, picks, small_sem, stage_sem, out_sem, ring_out_sem, qg_sem, a_sem, l_sem, r_sem, f_sem, s_sem,
                 twin_out, back_out, od_send, kv_send, twin_sem, hop_sem, bl_sem, br_sem, od_sem, kv_sem):
    z, x, c, y = places()
    zs = [(z + d) % NZ for d in range(NZ)]
    ys = [(y + d) % NY for d in range(NY)]
    right, left, over = (x + 1) % NX, (x + 3) % NX, (x + 2) % NX
    place = x * NC + c
    head = z * NY + y
    loads = [
        pltpu.make_async_copy(src, stage.at[n], stage_sem.at[n])
        for n, src in ((2, k_ref), (3, v_ref), (0, q_ref), (1, g_ref))
    ]
    small = [
        pltpu.make_async_copy(rand_hbm, rand, small_sem.at[0]),
        pltpu.make_async_copy(glob_hbm, glob, small_sem.at[1]),
    ]
    for load in loads + small:
        load.start()
    greet(z, x, c, y, zs, ys)

    def scatter(d, first, dst, sem):
        for n in range(NY):
            part = stage.at[pl.ds(first, 2), :, columns(zs[d], ys[n])]
            if d == 0 and n == 0:
                pltpu.make_async_copy(part, dst, sem).start()
            else:
                pltpu.make_async_remote_copy(
                    src_ref=part, dst_ref=dst, send_sem=out_sem, recv_sem=sem,
                    device_id=(zs[d], x, c, ys[n]), device_id_type=MESH,
                ).start()

    def chunk(zz, xx, cc):
        return kv.at[:, pl.ds(zz * 16 + xx * 4 + cc * 2, 2)]

    loads[0].wait()
    loads[1].wait()
    for d in ORDER:
        scatter(d, 2, kv.at[:, z * 16 + place * 2 + y // 2, quarter(y % 2), :], a_sem.at[z])

    small[0].wait()
    small[1].wait()
    lane = lax.broadcasted_iota(jnp.int32, (HEAD_DIM, HEAD_DIM), 1)
    row = lax.broadcasted_iota(jnp.int32, (HEAD_DIM, HEAD_DIM), 0)

    def names(slot):
        out = jnp.where(slot < WINDOW_TERMS, slot // NEAR * 16 + place * 2 - 1 + slot % NEAR, FAR)
        for plane in range(NZ):
            for n in range(2):
                for r in range(RANDS):
                    at = WINDOW_TERMS + (plane * 2 + n) * RANDS + r
                    out = jnp.where(slot == at, rand[r, head, plane * 16 + place * 2 + n], out)
        for n in range(2):
            out = jnp.where(slot == TERMS - 2 + n, glob[n], out)
        return out

    down = names(row)
    across = jnp.broadcast_to(names(lax.broadcasted_iota(jnp.int32, (1, HEAD_DIM), 1)), (HEAD_DIM, HEAD_DIM))
    ahead = (across < down) | ((across == down) & (lane < row))
    rank = jnp.sum(jnp.where(ahead, 1, 0), axis=1, keepdims=True)
    table[...] = jnp.zeros((8, HEAD_DIM), jnp.int32)
    table[0:1, :] = jnp.sum(jnp.where(rank == lane, row, 0), axis=0, keepdims=True)
    table[1:2, :] = jnp.sum(jnp.where(down < lane, 1, 0), axis=0, keepdims=True)
    table[2:3, :] = jnp.sum(jnp.where(down < lane + 1, 1, 0), axis=0, keepdims=True)
    picked = pltpu.make_async_copy(table, picks, small_sem.at[0])
    picked.start()
    terms[TERMS - 2] = jnp.zeros((2, BLOCK, HEAD_DIM), jnp.float32)
    terms[TERMS - 1] = jnp.zeros((2, BLOCK, HEAD_DIM), jnp.float32)
    picked.wait()
    loads[2].wait()
    loads[3].wait()

    def send(zz, xx, to, sem):
        pltpu.make_async_remote_copy(
            src_ref=chunk(zz, xx, c), dst_ref=chunk(zz, xx, c), send_sem=ring_out_sem, recv_sem=sem,
            device_id=to, device_id_type=MESH,
        ).start()

    to_right, to_left, to_twin = (z, right, c, y), (z, left, c, y), (z, x, 1 - c, y)
    source = [zs[(NZ - d) % NZ] for d in ORDER]
    for step in range(NZ + LAG2):
        if step < NZ:
            zz = source[step]
            drain(chunk(zz, x, c), a_sem.at[zz])
            send(zz, x, to_right, l_sem.at[zz])
            send(zz, x, to_left, r_sem.at[zz])
            send(zz, x, to_twin, s_sem)
            scatter(QORDER[step], 0, qg.at[:, z, quarter(y), :], qg_sem.at[z])
        if LAG1 <= step < NZ + LAG1:
            k = step - LAG1
            zz = source[k]
            drain(chunk(zz, left, c), l_sem.at[zz])
            if k % 2 == 1:
                send(zz, left, to_right, f_sem.at[zz])
            send(zz, left, to_twin, s_sem)
            drain(chunk(zz, right, c), r_sem.at[zz])
            if k % 2 == 0:
                send(zz, right, to_left, f_sem.at[zz])
            send(zz, right, to_twin, s_sem)
        if step >= LAG2:
            zz = source[step - LAG2]
            drain(chunk(zz, over, c), f_sem.at[zz])
            send(zz, over, to_twin, s_sem)
    drain(kv.at[:, pl.ds(0, BLOCKS // 2)], s_sem)

    def give(d, src, dst, send_sem, sem):
        for n in range(NY):
            part = src.at[:, quarter(ys[n]), :]
            if d == 0 and n == 0:
                pltpu.make_async_copy(part, dst.at[:, :, columns(z, y)], sem).start()
            else:
                pltpu.make_async_remote_copy(
                    src_ref=part, dst_ref=dst.at[:, :, columns(z, y)], send_sem=send_sem, recv_sem=sem,
                    device_id=(zs[d], x, c, ys[n]), device_id_type=MESH,
                ).start()

    shared = (NEAR + 2) * BLOCK
    every = shared + RANDS * BLOCK
    pair = 2 * BLOCK
    which = lax.broadcasted_iota(jnp.int32, (pair, every), 1) // BLOCK
    second = lax.broadcasted_iota(jnp.int32, (pair, every), 0) // BLOCK
    planes = [zs[d] for d in BACK]
    for turn in range(NZ // TURN):
        R = range(TURN)
        group = [planes[turn * TURN + n] for n in R]
        q, g, k, v, kr, vr = [], [], [], [], [], []
        for p in group:
            drain(qg.at[:, p], qg_sem.at[p])
            q.append(qg[0, p])
            g.append(qg[1, p])
            first = p * 16 + place * 2
            near = [(first + BLOCKS - 1) % BLOCKS, first, first + 1, (first + 2) % BLOCKS, glob[0], glob[1]]
            far = [[rand[r, head, first + n] for r in range(RANDS)] for n in range(2)]
            k.append(jnp.concatenate([kv[0, b] for b in near], axis=0))
            v.append(jnp.concatenate([kv[1, b] for b in near], axis=0))
            kr.append([jnp.concatenate([kv[0, b] for b in f], axis=0) for f in far])
            vr.append([jnp.concatenate([kv[1, b] for b in f], axis=0) for f in far])

        def halves(a):
            return a[:BLOCK], a[BLOCK:]

        def against(a, b, br):
            alone = jnp.concatenate([dot(h, m, NT) for h, m in zip(halves(a), br)], axis=0)
            return jnp.concatenate([dot(a, b, NT), alone], axis=1)

        def gathered(a, b, br):
            alone = jnp.concatenate([dot(h, m) for h, m in zip(halves(a[:, shared:]), br)], axis=0)
            return dot(a[:, :shared], b) + alone

        s = [against(q[n], k[n], kr[n]) for n in R]
        dp = [against(g[n], v[n], vr[n]) for n in R]
        p_, w, o, ds = [], [], [], []
        for n in R:
            first = group[n] * 16 + place * 2
            gone = (which == 0) & ((second == 1) | (first == 0))
            gone = gone | ((which == 3) & ((second == 0) | (first == BLOCKS - 2)))
            t = jnp.where(gone, -jnp.inf, s[n] * SCALE)
            e = jnp.exp(t - jnp.max(t, axis=1, keepdims=True))
            p_.append(e * (1.0 / jnp.sum(e, axis=1, keepdims=True)))
            w.append(narrow(p_[n]))
        for n in R:
            o.append(narrow(gathered(w[n], v[n], vr[n])))
        for n in R:
            delta = jnp.sum(wide(g[n]) * wide(o[n]), axis=1, keepdims=True)
            ds.append(narrow(p_[n] * (dp[n] - delta)))
        for n in R:
            p = group[n]
            for kind, left_, right_, scale in ((0, ds[n], q[n], SCALE), (1, w[n], g[n], 1.0)):
                both = dot(left_[:, :shared], right_, TN)
                for i in range(NEAR):
                    terms[p * NEAR + i, kind] = scale * both[i * BLOCK:(i + 1) * BLOCK]
                for i in range(2):
                    terms[TERMS - 2 + i, kind] += scale * both[(NEAR + i) * BLOCK:(NEAR + i + 1) * BLOCK]
                for h, (a, b) in enumerate(zip(halves(left_[:, shared:]), halves(right_))):
                    alone = scale * dot(a, b, TN)
                    for r in range(RANDS):
                        at = WINDOW_TERMS + (p * 2 + h) * RANDS + r
                        terms[at, kind] = alone[r * BLOCK:(r + 1) * BLOCK]
        for n in R:
            od[group[n], 0] = o[n]
            od[group[n], 1] = narrow(SCALE * gathered(ds[n], k[n], kr[n]))
            give(BACK[turn * TURN + n], od.at[group[n]], od_out, od_send, od_sem)

    total[0] = jnp.zeros((2, BLOCK, HEAD_DIM), jnp.float32)

    def run(n, carry):
        at = picks[0, n]
        carry = (carry[0] + terms[at, 0], carry[1] + terms[at, 1])
        total[n + 1, 0] = carry[0]
        total[n + 1, 1] = carry[1]
        return carry

    nothing = jnp.zeros((BLOCK, HEAD_DIM), jnp.float32)
    lax.fori_loop(0, TERMS, run, (nothing, nothing))

    def partial(kind, zz, xx, cc, half):
        block = zz * 16 + xx * 4 + cc * 2 + half
        return total[picks[2, block], kind] - total[picks[1, block], kind]

    for step in range(NZ):
        def fill(xx, carry, step=step):
            for kind in range(2):
                for half in range(2):
                    twin_send[step, kind, xx, half * BLOCK:(half + 1) * BLOCK, :] = narrow(
                        partial(kind, planes[step], xx, 1 - c, half)
                    )
            return carry

        lax.fori_loop(0, NX, fill, 0)
        pltpu.make_async_remote_copy(
            src_ref=twin_send.at[step], dst_ref=twin.at[step], send_sem=twin_out, recv_sem=twin_sem.at[step],
            device_id=to_twin, device_id_type=MESH,
        ).start()

    def pass_on(src, dst, sem, to):
        pltpu.make_async_remote_copy(
            src_ref=src, dst_ref=dst, send_sem=back_out, recv_sem=sem, device_id=to, device_id_type=MESH,
        ).start()

    for step in range(NZ + BACK2):
        if step < NZ:
            drain(twin.at[step], twin_sem.at[step])

            def add(xx, carry, step=step):
                for kind in range(2):
                    for half in range(2):
                        rows = slice(half * BLOCK, (half + 1) * BLOCK)
                        sums[step, kind, xx, rows, :] = narrow(
                            partial(kind, planes[step], xx, c, half) + wide(twin[step, kind, xx, rows, :])
                        )
                return carry

            lax.fori_loop(0, NX, add, 0)
            if step % 2 == 0:
                pass_on(sums.at[step, :, over], hop.at[step], hop_sem.at[step], to_right)
                pass_on(sums.at[step, :, left], from_right.at[step], br_sem.at[step], to_left)
            else:
                pass_on(sums.at[step, :, over], hop.at[step], hop_sem.at[step], to_left)
                pass_on(sums.at[step, :, right], from_left.at[step], bl_sem.at[step], to_right)
        if BACK1 <= step < NZ + BACK1:
            k = step - BACK1
            drain(hop.at[k], hop_sem.at[k])
            to = right if k % 2 == 0 else left
            for n in range(2):
                joined[k, n] = narrow(wide(sums[k, n, to]) + wide(hop[k, n]))
            if k % 2 == 0:
                pass_on(joined.at[k], from_left.at[k], bl_sem.at[k], to_right)
            else:
                pass_on(joined.at[k], from_right.at[k], br_sem.at[k], to_left)
        if step >= BACK2:
            k = step - BACK2
            drain(from_left.at[k], bl_sem.at[k])
            drain(from_right.at[k], br_sem.at[k])
            for n in range(2):
                final[k, n] = narrow(wide(sums[k, n, x]) + wide(from_left[k, n]) + wide(from_right[k, n]))
            give(BACK[k], final.at[k], dkv_out, kv_send, kv_sem)
    others = pl.ds(0, (NZ * NY - 1) * HEAD_DIM)
    drain(stage.at[:, :, others], out_sem)
    drain(kv.at[:, pl.ds(0, BLOCKS - 16)], ring_out_sem)
    drain(twin_send, twin_out)
    drain(sums.at[:, :, pl.ds(0, NX - 1)], back_out)
    drain(od_out.at[:, :, others], od_send)
    drain(dkv_out.at[:, :, others], kv_send)
    drain(od_out, od_sem)
    drain(dkv_out, kv_sem)


def layer(rand, glob, q, g, k, v):
    dma = pltpu.SemaphoreType.DMA
    hbm = pl.BlockSpec(memory_space=pltpu.HBM)
    anywhere = pl.BlockSpec(memory_space=pl.ANY)
    rows = jax.ShapeDtypeStruct((2, ROWS, WIDTH), jnp.bfloat16)
    half = jnp.bfloat16
    plane = pltpu.VMEM((NZ, 2, NY * ROWS, HEAD_DIM), half)
    planes = pltpu.VMEM((NZ, 2, NX, NY * ROWS, HEAD_DIM), half)
    each = dma((NZ,))
    return pl.pallas_call(
        layer_kernel,
        out_shape=(rows, rows),
        in_specs=[hbm] * 6,
        out_specs=(anywhere, anywhere),
        scratch_shapes=[
            pltpu.VMEM((4, ROWS, WIDTH), half),
            pltpu.VMEM((2, BLOCKS, BLOCK, HEAD_DIM), half),
            pltpu.VMEM((2, NZ, NY * ROWS, HEAD_DIM), half),
            plane,
            pltpu.VMEM((TERMS, 2, BLOCK, HEAD_DIM), jnp.float32),
            pltpu.VMEM((TERMS + 1, 2, BLOCK, HEAD_DIM), jnp.float32),
            pltpu.VMEM((8, HEAD_DIM), jnp.int32),
            planes, planes, planes, plane, plane, plane, plane, plane,
            pltpu.SMEM(rand.shape, jnp.int32),
            pltpu.SMEM(glob.shape, jnp.int32),
            pltpu.SMEM((8, HEAD_DIM), jnp.int32),
            dma((2,)), dma((4,)), dma, dma, each, each, each, each, each, dma,
            dma, dma, dma, dma, each, each, each, each, dma, dma,
        ],
        compiler_params=pltpu.CompilerParams(
            collective_id=0, has_side_effects=True, vmem_limit_bytes=48 * 1024 * 1024
        ),
    )(*(pltpu.with_memory_space_constraint(a, pltpu.HBM) for a in (rand, glob, q, g, k, v)))


def body(queries, keys, values, grad_out, random_blocks, global_blocks):
    rand = jnp.transpose(random_blocks, (2, 0, 1))
    od, dkv = layer(rand, global_blocks, queries, grad_out, keys, values)
    return od[0], od[1], dkv[0], dkv[1]


def solution(mesh):
    fine = jax.sharding.Mesh(mesh.devices.reshape(NZ, NX, NC, NY), ("z", "x", "core", "head"))
    rows = P(("z", "x", "core", "head"), None)
    return jax.shard_map(
        body,
        mesh=fine,
        in_specs=(rows, rows, rows, rows, P(), P()),
        out_specs=(rows, rows, rows, rows),
        check_vma=False,
    )
```

```python
import functools
import jax
import jax.numpy as jnp
from jax import lax
from jax.experimental import pallas as pl
from jax.experimental.pallas import tpu as pltpu
from jax.sharding import PartitionSpec as P

HEAD_DIM = 128
BLOCK = 64
SCALE = HEAD_DIM ** -0.5
BLOCKS = 128
MESH = pl.DeviceIdType.MESH
NZ, NX, NC, NY = 8, 4, 2, 4
ROWS = 32
WIDTH = 4096
ORDER = (0, 1, 7, 2, 6, 3, 5, 4)
BACK = (4, 3, 5, 2, 6, 1, 7, 0)
QORDER = (3, 5, 2, 6, 4, 1, 7, 0)
LAG1, LAG2 = 4, 8
BACK1, BACK2 = 2, 4
TABLES_AT = 8
AHEAD = 2
TURN = 4
NEAR = 4
RANDS = 3
WINDOW_TERMS = NZ * NEAR
TERMS = WINDOW_TERMS + NZ * 2 * RANDS + 2
FAR = 1000
NT = (((1,), (1,)), ((), ()))
TN = (((0,), (0,)), ((), ()))


def dot(a, b, dims=(((1,), (0,)), ((), ()))):
    return lax.dot_general(a, b, dims, preferred_element_type=jnp.float32)


def wide(a):
    return a.astype(jnp.float32)


def narrow(a):
    return a.astype(jnp.bfloat16)


def places():
    return tuple(lax.axis_index(a) for a in ("z", "x", "core", "head"))


def greet(z, x, c, y, zs, ys):
    barrier = pltpu.get_barrier_semaphore()

    def hello(zz, xx, cc, yy):
        pl.semaphore_signal(barrier, inc=1, device_id=(zz, xx, cc, yy), device_id_type=MESH)

    hello(z, x, 1 - c, y)
    hello(z, (x + 1) % NX, c, y)
    hello(z, (x + 3) % NX, c, y)
    for n in range(1, NZ * NY):
        hello(zs[n // NY], x, c, ys[n % NY])
    pl.semaphore_wait(barrier, NZ * NY - 1 + 3)


def drain(like, sem):
    pltpu.make_async_copy(like, like, sem).wait()


def columns(zz, yy):
    return pl.ds(pl.multiple_of((zz * NY + yy) * HEAD_DIM, HEAD_DIM), HEAD_DIM)


def quarter(yy):
    return pl.ds(pl.multiple_of(yy * ROWS, ROWS), ROWS)


def layer_kernel(rand_hbm, glob_hbm, q_ref, g_ref, k_ref, v_ref, od_out, dkv_out,
                 stage, kv, qg, od, terms, total, table, twin_send, twin, sums, hop, joined, from_left, from_right, final,
                 rand, glob, picks, small_sem, stage_sem, out_sem, ring_out_sem, qg_sem, a_sem, l_sem, r_sem, f_sem, s_sem,
                 twin_out, back_out, od_send, kv_send, twin_sem, hop_sem, bl_sem, br_sem, od_sem, kv_sem):
    z, x, c, y = places()
    zs = [(z + d) % NZ for d in range(NZ)]
    ys = [(y + d) % NY for d in range(NY)]
    right, left, over = (x + 1) % NX, (x + 3) % NX, (x + 2) % NX
    place = x * NC + c
    head = z * NY + y
    loads = [
        pltpu.make_async_copy(src, stage.at[n], stage_sem.at[n])
        for n, src in ((2, k_ref), (3, v_ref), (0, q_ref), (1, g_ref))
    ]
    small = [
        pltpu.make_async_copy(rand_hbm, rand, small_sem.at[0]),
        pltpu.make_async_copy(glob_hbm, glob, small_sem.at[1]),
    ]
    for load in loads + small:
        load.start()
    greet(z, x, c, y, zs, ys)

    def scatter(d, first, dst, sem):
        for n in range(NY):
            part = stage.at[pl.ds(first, 2), :, columns(zs[d], ys[n])]
            if d == 0 and n == 0:
                pltpu.make_async_copy(part, dst, sem).start()
            else:
                pltpu.make_async_remote_copy(
                    src_ref=part, dst_ref=dst, send_sem=out_sem, recv_sem=sem,
                    device_id=(zs[d], x, c, ys[n]), device_id_type=MESH,
                ).start()

    def chunk(zz, xx, cc):
        return kv.at[:, pl.ds(zz * 16 + xx * 4 + cc * 2, 2)]

    loads[0].wait()
    loads[1].wait()
    for d in ORDER:
        scatter(d, 2, kv.at[:, z * 16 + place * 2 + y // 2, quarter(y % 2), :], a_sem.at[z])

    loads[2].wait()
    loads[3].wait()

    picked = pltpu.make_async_copy(table, picks, small_sem.at[0])

    def order_terms():
        small[0].wait()
        small[1].wait()
        lane = lax.broadcasted_iota(jnp.int32, (HEAD_DIM, HEAD_DIM), 1)
        row = lax.broadcasted_iota(jnp.int32, (HEAD_DIM, HEAD_DIM), 0)

        def names(slot):
            out = jnp.where(slot < WINDOW_TERMS, slot // NEAR * 16 + place * 2 - 1 + slot % NEAR, FAR)
            for plane in range(NZ):
                for n in range(2):
                    for r in range(RANDS):
                        at = WINDOW_TERMS + (plane * 2 + n) * RANDS + r
                        out = jnp.where(slot == at, rand[r, head, plane * 16 + place * 2 + n], out)
            for n in range(2):
                out = jnp.where(slot == TERMS - 2 + n, glob[n], out)
            return out

        down = names(row)
        across = jnp.broadcast_to(names(lax.broadcasted_iota(jnp.int32, (1, HEAD_DIM), 1)), (HEAD_DIM, HEAD_DIM))
        ahead = (across < down) | ((across == down) & (lane < row))
        rank = jnp.sum(jnp.where(ahead, 1, 0), axis=1, keepdims=True)
        table[...] = jnp.zeros((8, HEAD_DIM), jnp.int32)
        table[0:1, :] = jnp.sum(jnp.where(rank == lane, row, 0), axis=0, keepdims=True)
        table[1:2, :] = jnp.sum(jnp.where(down < lane, 1, 0), axis=0, keepdims=True)
        table[2:3, :] = jnp.sum(jnp.where(down < lane + 1, 1, 0), axis=0, keepdims=True)
        picked.start()
        terms[TERMS - 2] = jnp.zeros((2, BLOCK, HEAD_DIM), jnp.float32)
        terms[TERMS - 1] = jnp.zeros((2, BLOCK, HEAD_DIM), jnp.float32)

    def send(zz, xx, to, sem):
        pltpu.make_async_remote_copy(
            src_ref=chunk(zz, xx, c), dst_ref=chunk(zz, xx, c), send_sem=ring_out_sem, recv_sem=sem,
            device_id=to, device_id_type=MESH,
        ).start()

    to_right, to_left, to_twin = (z, right, c, y), (z, left, c, y), (z, x, 1 - c, y)
    source = [zs[(NZ - d) % NZ] for d in ORDER]
    for step in range(NZ + LAG2):
        if step == TABLES_AT:
            order_terms()
        if step < NZ:
            zz = source[step]
            drain(chunk(zz, x, c), a_sem.at[zz])
            send(zz, x, to_right, l_sem.at[zz])
            send(zz, x, to_left, r_sem.at[zz])
            send(zz, x, to_twin, s_sem)
            scatter(QORDER[step], 0, qg.at[:, z, quarter(y), :], qg_sem.at[z])
        if LAG1 <= step < NZ + LAG1:
            k = step - LAG1
            zz = source[k]
            drain(chunk(zz, left, c), l_sem.at[zz])
            if k % 2 == 1:
                send(zz, left, to_right, f_sem.at[zz])
            send(zz, left, to_twin, s_sem)
            drain(chunk(zz, right, c), r_sem.at[zz])
            if k % 2 == 0:
                send(zz, right, to_left, f_sem.at[zz])
            send(zz, right, to_twin, s_sem)
        if step >= LAG2:
            zz = source[step - LAG2]
            drain(chunk(zz, over, c), f_sem.at[zz])
            send(zz, over, to_twin, s_sem)
    drain(kv.at[:, pl.ds(0, BLOCKS // 2)], s_sem)

    def give(d, src, dst, send_sem, sem):
        for n in range(NY):
            part = src.at[:, quarter(ys[n]), :]
            if d == 0 and n == 0:
                pltpu.make_async_copy(part, dst.at[:, :, columns(z, y)], sem).start()
            else:
                pltpu.make_async_remote_copy(
                    src_ref=part, dst_ref=dst.at[:, :, columns(z, y)], send_sem=send_sem, recv_sem=sem,
                    device_id=(zs[d], x, c, ys[n]), device_id_type=MESH,
                ).start()

    shared = (NEAR + 2) * BLOCK
    every = shared + RANDS * BLOCK
    pair = 2 * BLOCK
    which = lax.broadcasted_iota(jnp.int32, (pair, every), 1) // BLOCK
    second = lax.broadcasted_iota(jnp.int32, (pair, every), 0) // BLOCK
    planes = [zs[d] for d in BACK]
    for turn in range(NZ // TURN):
        R = range(TURN)
        group = [planes[turn * TURN + n] for n in R]
        q, g, k, v, kr, vr = [], [], [], [], [], []
        for p in group:
            drain(qg.at[:, p], qg_sem.at[p])
            q.append(qg[0, p])
            g.append(qg[1, p])
            first = p * 16 + place * 2
            near = [(first + BLOCKS - 1) % BLOCKS, first, first + 1, (first + 2) % BLOCKS, glob[0], glob[1]]
            far = [[rand[r, head, first + n] for r in range(RANDS)] for n in range(2)]
            k.append(jnp.concatenate([kv[0, b] for b in near], axis=0))
            v.append(jnp.concatenate([kv[1, b] for b in near], axis=0))
            kr.append([jnp.concatenate([kv[0, b] for b in f], axis=0) for f in far])
            vr.append([jnp.concatenate([kv[1, b] for b in f], axis=0) for f in far])

        def halves(a):
            return a[:BLOCK], a[BLOCK:]

        def against(a, b, br):
            alone = jnp.concatenate([dot(h, m, NT) for h, m in zip(halves(a), br)], axis=0)
            return jnp.concatenate([dot(a, b, NT), alone], axis=1)

        def gathered(a, b, br):
            alone = jnp.concatenate([dot(h, m) for h, m in zip(halves(a[:, shared:]), br)], axis=0)
            return dot(a[:, :shared], b) + alone

        s = [against(q[n], k[n], kr[n]) for n in R]
        dp = [against(g[n], v[n], vr[n]) for n in R]
        p_, w, o, ds = [], [], [], []
        for n in R:
            first = group[n] * 16 + place * 2
            gone = (which == 0) & ((second == 1) | (first == 0))
            gone = gone | ((which == 3) & ((second == 0) | (first == BLOCKS - 2)))
            t = jnp.where(gone, -jnp.inf, s[n] * SCALE)
            e = jnp.exp(t - jnp.max(t, axis=1, keepdims=True))
            p_.append(e * (1.0 / jnp.sum(e, axis=1, keepdims=True)))
            w.append(narrow(p_[n]))
        for n in R:
            o.append(narrow(gathered(w[n], v[n], vr[n])))
        for n in R:
            delta = jnp.sum(wide(g[n]) * wide(o[n]), axis=1, keepdims=True)
            ds.append(narrow(p_[n] * (dp[n] - delta)))
        for n in R:
            p = group[n]
            for kind, left_, right_, scale in ((0, ds[n], q[n], SCALE), (1, w[n], g[n], 1.0)):
                both = dot(left_[:, :shared], right_, TN)
                for i in range(NEAR):
                    terms[p * NEAR + i, kind] = scale * both[i * BLOCK:(i + 1) * BLOCK]
                for i in range(2):
                    terms[TERMS - 2 + i, kind] += scale * both[(NEAR + i) * BLOCK:(NEAR + i + 1) * BLOCK]
                for h, (a, b) in enumerate(zip(halves(left_[:, shared:]), halves(right_))):
                    alone = scale * dot(a, b, TN)
                    for r in range(RANDS):
                        at = WINDOW_TERMS + (p * 2 + h) * RANDS + r
                        terms[at, kind] = alone[r * BLOCK:(r + 1) * BLOCK]
        for n in R:
            od[group[n], 0] = o[n]
            od[group[n], 1] = narrow(SCALE * gathered(ds[n], k[n], kr[n]))
            give(BACK[turn * TURN + n], od.at[group[n]], od_out, od_send, od_sem)

    picked.wait()

    total[0] = jnp.zeros((2, BLOCK, HEAD_DIM), jnp.float32)

    def run(n, carry):
        at = picks[0, n]
        carry = (carry[0] + terms[at, 0], carry[1] + terms[at, 1])
        total[n + 1, 0] = carry[0]
        total[n + 1, 1] = carry[1]
        return carry

    nothing = jnp.zeros((BLOCK, HEAD_DIM), jnp.float32)
    lax.fori_loop(0, TERMS, run, (nothing, nothing))

    def partial(kind, zz, xx, cc, half):
        block = zz * 16 + xx * 4 + cc * 2 + half
        return total[picks[2, block], kind] - total[picks[1, block], kind]

    def fill_twin(step):
        def fill(xx, carry):
            for kind in range(2):
                for half in range(2):
                    twin_send[step, kind, xx, half * BLOCK:(half + 1) * BLOCK, :] = narrow(
                        partial(kind, planes[step], xx, 1 - c, half)
                    )
            return carry

        lax.fori_loop(0, NX, fill, 0)
        pltpu.make_async_remote_copy(
            src_ref=twin_send.at[step], dst_ref=twin.at[step], send_sem=twin_out, recv_sem=twin_sem.at[step],
            device_id=to_twin, device_id_type=MESH,
        ).start()

    for step in range(AHEAD):
        fill_twin(step)

    def pass_on(src, dst, sem, to):
        pltpu.make_async_remote_copy(
            src_ref=src, dst_ref=dst, send_sem=back_out, recv_sem=sem, device_id=to, device_id_type=MESH,
        ).start()

    for step in range(NZ + BACK2):
        if step < NZ - AHEAD:
            fill_twin(step + AHEAD)
        if step < NZ:
            drain(twin.at[step], twin_sem.at[step])

            def add(xx, carry, step=step):
                for kind in range(2):
                    for half in range(2):
                        rows = slice(half * BLOCK, (half + 1) * BLOCK)
                        sums[step, kind, xx, rows, :] = narrow(
                            partial(kind, planes[step], xx, c, half) + wide(twin[step, kind, xx, rows, :])
                        )
                return carry

            lax.fori_loop(0, NX, add, 0)
            if step % 2 == 0:
                pass_on(sums.at[step, :, over], hop.at[step], hop_sem.at[step], to_right)
                pass_on(sums.at[step, :, left], from_right.at[step], br_sem.at[step], to_left)
            else:
                pass_on(sums.at[step, :, over], hop.at[step], hop_sem.at[step], to_left)
                pass_on(sums.at[step, :, right], from_left.at[step], bl_sem.at[step], to_right)
        if BACK1 <= step < NZ + BACK1:
            k = step - BACK1
            drain(hop.at[k], hop_sem.at[k])
            to = right if k % 2 == 0 else left
            for n in range(2):
                joined[k, n] = narrow(wide(sums[k, n, to]) + wide(hop[k, n]))
            if k % 2 == 0:
                pass_on(joined.at[k], from_left.at[k], bl_sem.at[k], to_right)
            else:
                pass_on(joined.at[k], from_right.at[k], br_sem.at[k], to_left)
        if step >= BACK2:
            k = step - BACK2
            drain(from_left.at[k], bl_sem.at[k])
            drain(from_right.at[k], br_sem.at[k])
            for n in range(2):
                final[k, n] = narrow(wide(sums[k, n, x]) + wide(from_left[k, n]) + wide(from_right[k, n]))
            give(BACK[k], final.at[k], dkv_out, kv_send, kv_sem)
    others = pl.ds(0, (NZ * NY - 1) * HEAD_DIM)
    drain(stage.at[:, :, others], out_sem)
    drain(kv.at[:, pl.ds(0, BLOCKS - 16)], ring_out_sem)
    drain(twin_send, twin_out)
    drain(sums.at[:, :, pl.ds(0, NX - 1)], back_out)
    drain(od_out.at[:, :, others], od_send)
    drain(dkv_out.at[:, :, others], kv_send)
    drain(od_out, od_sem)
    drain(dkv_out, kv_sem)


def layer(rand, glob, q, g, k, v):
    dma = pltpu.SemaphoreType.DMA
    hbm = pl.BlockSpec(memory_space=pltpu.HBM)
    anywhere = pl.BlockSpec(memory_space=pl.ANY)
    rows = jax.ShapeDtypeStruct((2, ROWS, WIDTH), jnp.bfloat16)
    half = jnp.bfloat16
    plane = pltpu.VMEM((NZ, 2, NY * ROWS, HEAD_DIM), half)
    planes = pltpu.VMEM((NZ, 2, NX, NY * ROWS, HEAD_DIM), half)
    each = dma((NZ,))
    return pl.pallas_call(
        layer_kernel,
        out_shape=(rows, rows),
        in_specs=[hbm] * 6,
        out_specs=(anywhere, anywhere),
        scratch_shapes=[
            pltpu.VMEM((4, ROWS, WIDTH), half),
            pltpu.VMEM((2, BLOCKS, BLOCK, HEAD_DIM), half),
            pltpu.VMEM((2, NZ, NY * ROWS, HEAD_DIM), half),
            plane,
            pltpu.VMEM((TERMS, 2, BLOCK, HEAD_DIM), jnp.float32),
            pltpu.VMEM((TERMS + 1, 2, BLOCK, HEAD_DIM), jnp.float32),
            pltpu.VMEM((8, HEAD_DIM), jnp.int32),
            planes, planes, planes, plane, plane, plane, plane, plane,
            pltpu.SMEM(rand.shape, jnp.int32),
            pltpu.SMEM(glob.shape, jnp.int32),
            pltpu.SMEM((8, HEAD_DIM), jnp.int32),
            dma((2,)), dma((4,)), dma, dma, each, each, each, each, each, dma,
            dma, dma, dma, dma, each, each, each, each, dma, dma,
        ],
        compiler_params=pltpu.CompilerParams(
            collective_id=0, has_side_effects=True, vmem_limit_bytes=48 * 1024 * 1024
        ),
    )(*(pltpu.with_memory_space_constraint(a, pltpu.HBM) for a in (rand, glob, q, g, k, v)))


def body(queries, keys, values, grad_out, random_blocks, global_blocks):
    rand = jnp.transpose(random_blocks, (2, 0, 1))
    od, dkv = layer(rand, global_blocks, queries, grad_out, keys, values)
    return od[0], od[1], dkv[0], dkv[1]


def solution(mesh):
    fine = jax.sharding.Mesh(mesh.devices.reshape(NZ, NX, NC, NY), ("z", "x", "core", "head"))
    rows = P(("z", "x", "core", "head"), None)
    return jax.shard_map(
        body,
        mesh=fine,
        in_specs=(rows, rows, rows, rows, P(), P()),
        out_specs=(rows, rows, rows, rows),
        check_vma=False,
    )
```

```python
import functools
import jax
import jax.numpy as jnp
from jax import lax
from jax.experimental import pallas as pl
from jax.experimental.pallas import tpu as pltpu
from jax.sharding import PartitionSpec as P

HEAD_DIM = 128
BLOCK = 64
SCALE = HEAD_DIM ** -0.5
BLOCKS = 128
MESH = pl.DeviceIdType.MESH
NZ, NX, NC, NY = 8, 4, 2, 4
ROWS = 32
WIDTH = 4096
ORDER = (0, 1, 7, 2, 6, 3, 5, 4)
BACK = (4, 3, 5, 2, 6, 1, 7, 0)
QORDER = (3, 5, 2, 6, 4, 1, 7, 0)
LAG1, LAG2 = 4, 8
BACK1, BACK2 = 2, 4
TABLES_AT = 8
AHEAD = 2
TURN = 4
NEAR = 4
RANDS = 3
WINDOW_TERMS = NZ * NEAR
TERMS = WINDOW_TERMS + NZ * 2 * RANDS + 2
FAR = 1000
NT = (((1,), (1,)), ((), ()))
TN = (((0,), (0,)), ((), ()))


def dot(a, b, dims=(((1,), (0,)), ((), ()))):
    return lax.dot_general(a, b, dims, preferred_element_type=jnp.float32)


def wide(a):
    return a.astype(jnp.float32)


def narrow(a):
    return a.astype(jnp.bfloat16)


def places():
    return tuple(lax.axis_index(a) for a in ("z", "x", "core", "head"))


def greet(z, x, c, y, zs, ys):
    barrier = pltpu.get_barrier_semaphore()

    def hello(zz, xx, cc, yy):
        pl.semaphore_signal(barrier, inc=1, device_id=(zz, xx, cc, yy), device_id_type=MESH)

    hello(z, x, 1 - c, y)
    hello(z, (x + 1) % NX, c, y)
    hello(z, (x + 3) % NX, c, y)
    for n in range(1, NZ * NY):
        hello(zs[n // NY], x, c, ys[n % NY])
    pl.semaphore_wait(barrier, NZ * NY - 1 + 3)


def drain(like, sem):
    pltpu.make_async_copy(like, like, sem).wait()


def columns(zz, yy):
    return pl.ds(pl.multiple_of((zz * NY + yy) * HEAD_DIM, HEAD_DIM), HEAD_DIM)


def quarter(yy):
    return pl.ds(pl.multiple_of(yy * ROWS, ROWS), ROWS)


def layer_kernel(rand_hbm, glob_hbm, q_ref, g_ref, k_ref, v_ref, od_out, dkv_out,
                 stage, kv, qg, od, terms, total, table, twin_send, twin, sums, hop, joined, from_left, from_right, final,
                 rand, glob, picks, small_sem, stage_sem, out_sem, ring_out_sem, qg_sem, a_sem, l_sem, r_sem, f_sem, s_sem,
                 twin_out, back_out, od_send, kv_send, twin_sem, hop_sem, bl_sem, br_sem, od_sem, kv_sem):
    z, x, c, y = places()
    zs = [(z + d) % NZ for d in range(NZ)]
    ys = [(y + d) % NY for d in range(NY)]
    right, left, over = (x + 1) % NX, (x + 3) % NX, (x + 2) % NX
    place = x * NC + c
    head = z * NY + y
    loads = [
        pltpu.make_async_copy(src, stage.at[n], stage_sem.at[n])
        for n, src in ((2, k_ref), (3, v_ref), (0, q_ref), (1, g_ref))
    ]
    small = [
        pltpu.make_async_copy(rand_hbm, rand, small_sem.at[0]),
        pltpu.make_async_copy(glob_hbm, glob, small_sem.at[1]),
    ]
    for load in loads + small:
        load.start()
    greet(z, x, c, y, zs, ys)

    def scatter(d, first, dst, sem):
        for n in range(NY):
            part = stage.at[pl.ds(first, 2), :, columns(zs[d], ys[n])]
            if d == 0 and n == 0:
                pltpu.make_async_copy(part, dst, sem).start()
            else:
                pltpu.make_async_remote_copy(
                    src_ref=part, dst_ref=dst, send_sem=out_sem, recv_sem=sem,
                    device_id=(zs[d], x, c, ys[n]), device_id_type=MESH,
                ).start()

    def chunk(zz, xx, cc):
        return kv.at[:, pl.ds(zz * 16 + xx * 4 + cc * 2, 2)]

    loads[0].wait()
    loads[1].wait()
    for d in ORDER:
        scatter(d, 2, kv.at[:, z * 16 + place * 2 + y // 2, quarter(y % 2), :], a_sem.at[z])

    loads[2].wait()
    loads[3].wait()

    picked = pltpu.make_async_copy(table, picks, small_sem.at[0])

    def order_terms():
        small[0].wait()
        small[1].wait()
        lane = lax.broadcasted_iota(jnp.int32, (HEAD_DIM, HEAD_DIM), 1)
        row = lax.broadcasted_iota(jnp.int32, (HEAD_DIM, HEAD_DIM), 0)

        def names(slot):
            out = jnp.where(slot < WINDOW_TERMS, slot // NEAR * 16 + place * 2 - 1 + slot % NEAR, FAR)
            for plane in range(NZ):
                for n in range(2):
                    for r in range(RANDS):
                        at = WINDOW_TERMS + (plane * 2 + n) * RANDS + r
                        out = jnp.where(slot == at, rand[r, head, plane * 16 + place * 2 + n], out)
            for n in range(2):
                out = jnp.where(slot == TERMS - 2 + n, glob[n], out)
            return out

        down = names(row)
        across = jnp.broadcast_to(names(lax.broadcasted_iota(jnp.int32, (1, HEAD_DIM), 1)), (HEAD_DIM, HEAD_DIM))
        ahead = (across < down) | ((across == down) & (lane < row))
        rank = jnp.sum(jnp.where(ahead, 1, 0), axis=1, keepdims=True)
        table[...] = jnp.zeros((8, HEAD_DIM), jnp.int32)
        table[0:1, :] = jnp.sum(jnp.where(rank == lane, row, 0), axis=0, keepdims=True)
        table[1:2, :] = jnp.sum(jnp.where(down < lane, 1, 0), axis=0, keepdims=True)
        table[2:3, :] = jnp.sum(jnp.where(down < lane + 1, 1, 0), axis=0, keepdims=True)
        picked.start()
        terms[TERMS - 2] = jnp.zeros((2, BLOCK, HEAD_DIM), jnp.float32)
        terms[TERMS - 1] = jnp.zeros((2, BLOCK, HEAD_DIM), jnp.float32)

    def send(zz, xx, to, sem):
        pltpu.make_async_remote_copy(
            src_ref=chunk(zz, xx, c), dst_ref=chunk(zz, xx, c), send_sem=ring_out_sem, recv_sem=sem,
            device_id=to, device_id_type=MESH,
        ).start()

    to_right, to_left, to_twin = (z, right, c, y), (z, left, c, y), (z, x, 1 - c, y)
    source = [zs[(NZ - d) % NZ] for d in ORDER]
    for step in range(NZ + LAG2):
        if step == TABLES_AT:
            order_terms()
        if step < NZ:
            zz = source[step]
            drain(chunk(zz, x, c), a_sem.at[zz])
            send(zz, x, to_right, l_sem.at[zz])
            send(zz, x, to_left, r_sem.at[zz])
            send(zz, x, to_twin, s_sem)
            for d in QORDER[2 * step:2 * step + 2]:
                scatter(d, 0, qg.at[:, z, quarter(y), :], qg_sem.at[z])
        if LAG1 <= step < NZ + LAG1:
            k = step - LAG1
            zz = source[k]
            drain(chunk(zz, left, c), l_sem.at[zz])
            if k % 2 == 1:
                send(zz, left, to_right, f_sem.at[zz])
            send(zz, left, to_twin, s_sem)
            drain(chunk(zz, right, c), r_sem.at[zz])
            if k % 2 == 0:
                send(zz, right, to_left, f_sem.at[zz])
            send(zz, right, to_twin, s_sem)
        if step >= LAG2:
            zz = source[step - LAG2]
            drain(chunk(zz, over, c), f_sem.at[zz])
            send(zz, over, to_twin, s_sem)
    drain(kv.at[:, pl.ds(0, BLOCKS // 2)], s_sem)

    def give(d, src, dst, send_sem, sem):
        for n in range(NY):
            part = src.at[:, quarter(ys[n]), :]
            if d == 0 and n == 0:
                pltpu.make_async_copy(part, dst.at[:, :, columns(z, y)], sem).start()
            else:
                pltpu.make_async_remote_copy(
                    src_ref=part, dst_ref=dst.at[:, :, columns(z, y)], send_sem=send_sem, recv_sem=sem,
                    device_id=(zs[d], x, c, ys[n]), device_id_type=MESH,
                ).start()

    shared = (NEAR + 2) * BLOCK
    every = shared + RANDS * BLOCK
    pair = 2 * BLOCK
    which = lax.broadcasted_iota(jnp.int32, (pair, every), 1) // BLOCK
    second = lax.broadcasted_iota(jnp.int32, (pair, every), 0) // BLOCK
    planes = [zs[d] for d in BACK]
    for turn in range(NZ // TURN):
        R = range(TURN)
        group = [planes[turn * TURN + n] for n in R]
        q, g, k, v, kr, vr = [], [], [], [], [], []
        for p in group:
            drain(qg.at[:, p], qg_sem.at[p])
            q.append(qg[0, p])
            g.append(qg[1, p])
            first = p * 16 + place * 2
            near = [(first + BLOCKS - 1) % BLOCKS, first, first + 1, (first + 2) % BLOCKS, glob[0], glob[1]]
            far = [[rand[r, head, first + n] for r in range(RANDS)] for n in range(2)]
            k.append(jnp.concatenate([kv[0, b] for b in near], axis=0))
            v.append(jnp.concatenate([kv[1, b] for b in near], axis=0))
            kr.append([jnp.concatenate([kv[0, b] for b in f], axis=0) for f in far])
            vr.append([jnp.concatenate([kv[1, b] for b in f], axis=0) for f in far])

        def halves(a):
            return a[:BLOCK], a[BLOCK:]

        def against(a, b, br):
            alone = jnp.concatenate([dot(h, m, NT) for h, m in zip(halves(a), br)], axis=0)
            return jnp.concatenate([dot(a, b, NT), alone], axis=1)

        def gathered(a, b, br):
            alone = jnp.concatenate([dot(h, m) for h, m in zip(halves(a[:, shared:]), br)], axis=0)
            return dot(a[:, :shared], b) + alone

        s = [against(q[n], k[n], kr[n]) for n in R]
        dp = [against(g[n], v[n], vr[n]) for n in R]
        p_, w, o, ds = [], [], [], []
        for n in R:
            first = group[n] * 16 + place * 2
            gone = (which == 0) & ((second == 1) | (first == 0))
            gone = gone | ((which == 3) & ((second == 0) | (first == BLOCKS - 2)))
            t = jnp.where(gone, -jnp.inf, s[n] * SCALE)
            e = jnp.exp(t - jnp.max(t, axis=1, keepdims=True))
            p_.append(e * (1.0 / jnp.sum(e, axis=1, keepdims=True)))
            w.append(narrow(p_[n]))
        for n in R:
            o.append(narrow(gathered(w[n], v[n], vr[n])))
        for n in R:
            delta = jnp.sum(wide(g[n]) * wide(o[n]), axis=1, keepdims=True)
            ds.append(narrow(p_[n] * (dp[n] - delta)))
        for n in R:
            p = group[n]
            for kind, left_, right_, scale in ((0, ds[n], q[n], SCALE), (1, w[n], g[n], 1.0)):
                both = dot(left_[:, :shared], right_, TN)
                for i in range(NEAR):
                    terms[p * NEAR + i, kind] = scale * both[i * BLOCK:(i + 1) * BLOCK]
                for i in range(2):
                    terms[TERMS - 2 + i, kind] += scale * both[(NEAR + i) * BLOCK:(NEAR + i + 1) * BLOCK]
                for h, (a, b) in enumerate(zip(halves(left_[:, shared:]), halves(right_))):
                    alone = scale * dot(a, b, TN)
                    for r in range(RANDS):
                        at = WINDOW_TERMS + (p * 2 + h) * RANDS + r
                        terms[at, kind] = alone[r * BLOCK:(r + 1) * BLOCK]
        for n in R:
            od[group[n], 0] = o[n]
            od[group[n], 1] = narrow(SCALE * gathered(ds[n], k[n], kr[n]))
            give(BACK[turn * TURN + n], od.at[group[n]], od_out, od_send, od_sem)

    picked.wait()

    total[0] = jnp.zeros((2, BLOCK, HEAD_DIM), jnp.float32)

    def run(n, carry):
        at = picks[0, n]
        carry = (carry[0] + terms[at, 0], carry[1] + terms[at, 1])
        total[n + 1, 0] = carry[0]
        total[n + 1, 1] = carry[1]
        return carry

    nothing = jnp.zeros((BLOCK, HEAD_DIM), jnp.float32)
    lax.fori_loop(0, TERMS, run, (nothing, nothing))

    def partial(kind, zz, xx, cc, half):
        block = zz * 16 + xx * 4 + cc * 2 + half
        return total[picks[2, block], kind] - total[picks[1, block], kind]

    def fill_twin(step):
        def fill(xx, carry):
            for kind in range(2):
                for half in range(2):
                    twin_send[step, kind, xx, half * BLOCK:(half + 1) * BLOCK, :] = narrow(
                        partial(kind, planes[step], xx, 1 - c, half)
                    )
            return carry

        lax.fori_loop(0, NX, fill, 0)
        pltpu.make_async_remote_copy(
            src_ref=twin_send.at[step], dst_ref=twin.at[step], send_sem=twin_out, recv_sem=twin_sem.at[step],
            device_id=to_twin, device_id_type=MESH,
        ).start()

    for step in range(AHEAD):
        fill_twin(step)

    def pass_on(src, dst, sem, to):
        pltpu.make_async_remote_copy(
            src_ref=src, dst_ref=dst, send_sem=back_out, recv_sem=sem, device_id=to, device_id_type=MESH,
        ).start()

    for step in range(NZ + BACK2):
        if step < NZ - AHEAD:
            fill_twin(step + AHEAD)
        if step < NZ:
            drain(twin.at[step], twin_sem.at[step])

            def add(xx, carry, step=step):
                for kind in range(2):
                    for half in range(2):
                        rows = slice(half * BLOCK, (half + 1) * BLOCK)
                        sums[step, kind, xx, rows, :] = narrow(
                            partial(kind, planes[step], xx, c, half) + wide(twin[step, kind, xx, rows, :])
                        )
                return carry

            lax.fori_loop(0, NX, add, 0)
            if step % 2 == 0:
                pass_on(sums.at[step, :, over], hop.at[step], hop_sem.at[step], to_right)
                pass_on(sums.at[step, :, left], from_right.at[step], br_sem.at[step], to_left)
            else:
                pass_on(sums.at[step, :, over], hop.at[step], hop_sem.at[step], to_left)
                pass_on(sums.at[step, :, right], from_left.at[step], bl_sem.at[step], to_right)
        if BACK1 <= step < NZ + BACK1:
            k = step - BACK1
            drain(hop.at[k], hop_sem.at[k])
            to = right if k % 2 == 0 else left
            for n in range(2):
                joined[k, n] = narrow(wide(sums[k, n, to]) + wide(hop[k, n]))
            if k % 2 == 0:
                pass_on(joined.at[k], from_left.at[k], bl_sem.at[k], to_right)
            else:
                pass_on(joined.at[k], from_right.at[k], br_sem.at[k], to_left)
        if step >= BACK2:
            k = step - BACK2
            drain(from_left.at[k], bl_sem.at[k])
            drain(from_right.at[k], br_sem.at[k])
            for n in range(2):
                final[k, n] = narrow(wide(sums[k, n, x]) + wide(from_left[k, n]) + wide(from_right[k, n]))
            give(BACK[k], final.at[k], dkv_out, kv_send, kv_sem)
    others = pl.ds(0, (NZ * NY - 1) * HEAD_DIM)
    drain(stage.at[:, :, others], out_sem)
    drain(kv.at[:, pl.ds(0, BLOCKS - 16)], ring_out_sem)
    drain(twin_send, twin_out)
    drain(sums.at[:, :, pl.ds(0, NX - 1)], back_out)
    drain(od_out.at[:, :, others], od_send)
    drain(dkv_out.at[:, :, others], kv_send)
    drain(od_out, od_sem)
    drain(dkv_out, kv_sem)


def layer(rand, glob, q, g, k, v):
    dma = pltpu.SemaphoreType.DMA
    hbm = pl.BlockSpec(memory_space=pltpu.HBM)
    anywhere = pl.BlockSpec(memory_space=pl.ANY)
    rows = jax.ShapeDtypeStruct((2, ROWS, WIDTH), jnp.bfloat16)
    half = jnp.bfloat16
    plane = pltpu.VMEM((NZ, 2, NY * ROWS, HEAD_DIM), half)
    planes = pltpu.VMEM((NZ, 2, NX, NY * ROWS, HEAD_DIM), half)
    each = dma((NZ,))
    return pl.pallas_call(
        layer_kernel,
        out_shape=(rows, rows),
        in_specs=[hbm] * 6,
        out_specs=(anywhere, anywhere),
        scratch_shapes=[
            pltpu.VMEM((4, ROWS, WIDTH), half),
            pltpu.VMEM((2, BLOCKS, BLOCK, HEAD_DIM), half),
            pltpu.VMEM((2, NZ, NY * ROWS, HEAD_DIM), half),
            plane,
            pltpu.VMEM((TERMS, 2, BLOCK, HEAD_DIM), jnp.float32),
            pltpu.VMEM((TERMS + 1, 2, BLOCK, HEAD_DIM), jnp.float32),
            pltpu.VMEM((8, HEAD_DIM), jnp.int32),
            planes, planes, planes, plane, plane, plane, plane, plane,
            pltpu.SMEM(rand.shape, jnp.int32),
            pltpu.SMEM(glob.shape, jnp.int32),
            pltpu.SMEM((8, HEAD_DIM), jnp.int32),
            dma((2,)), dma((4,)), dma, dma, each, each, each, each, each, dma,
            dma, dma, dma, dma, each, each, each, each, dma, dma,
        ],
        compiler_params=pltpu.CompilerParams(
            collective_id=0, has_side_effects=True, vmem_limit_bytes=48 * 1024 * 1024
        ),
    )(*(pltpu.with_memory_space_constraint(a, pltpu.HBM) for a in (rand, glob, q, g, k, v)))


def body(queries, keys, values, grad_out, random_blocks, global_blocks):
    rand = jnp.transpose(random_blocks, (2, 0, 1))
    od, dkv = layer(rand, global_blocks, queries, grad_out, keys, values)
    return od[0], od[1], dkv[0], dkv[1]


def solution(mesh):
    fine = jax.sharding.Mesh(mesh.devices.reshape(NZ, NX, NC, NY), ("z", "x", "core", "head"))
    rows = P(("z", "x", "core", "head"), None)
    return jax.shard_map(
        body,
        mesh=fine,
        in_specs=(rows, rows, rows, rows, P(), P()),
        out_specs=(rows, rows, rows, rows),
        check_vma=False,
    )
```

```python
import functools
import jax
import jax.numpy as jnp
from jax import lax
from jax.experimental import pallas as pl
from jax.experimental.pallas import tpu as pltpu
from jax.sharding import PartitionSpec as P

HEAD_DIM = 128
BLOCK = 64
SCALE = HEAD_DIM ** -0.5
BLOCKS = 128
MESH = pl.DeviceIdType.MESH
NZ, NX, NC, NY = 8, 4, 2, 4
ROWS = 32
WIDTH = 4096
ORDER = (0, 1, 7, 2, 6, 3, 5, 4)
BACK = (4, 3, 5, 2, 6, 1, 7, 0)
QORDER = (3, 5, 2, 6, 4, 1, 7, 0)
LAG1, LAG2 = 4, 8
BACK1, BACK2 = 2, 4
TABLES_AT = 8
AHEAD = 2
TURN = 4
NEAR = 4
RANDS = 3
WINDOW_TERMS = NZ * NEAR
TERMS = WINDOW_TERMS + NZ * 2 * RANDS + 2
FAR = 1000
NT = (((1,), (1,)), ((), ()))
TN = (((0,), (0,)), ((), ()))


def dot(a, b, dims=(((1,), (0,)), ((), ()))):
    return lax.dot_general(a, b, dims, preferred_element_type=jnp.float32)


def wide(a):
    return a.astype(jnp.float32)


def narrow(a):
    return a.astype(jnp.bfloat16)


def places():
    return tuple(lax.axis_index(a) for a in ("z", "x", "core", "head"))


def greet(z, x, c, y, zs, ys):
    barrier = pltpu.get_barrier_semaphore()

    def hello(zz, xx, cc, yy):
        pl.semaphore_signal(barrier, inc=1, device_id=(zz, xx, cc, yy), device_id_type=MESH)

    hello(z, x, 1 - c, y)
    hello(z, (x + 1) % NX, c, y)
    hello(z, (x + 3) % NX, c, y)
    for n in range(1, NZ * NY):
        hello(zs[n // NY], x, c, ys[n % NY])
    pl.semaphore_wait(barrier, NZ * NY - 1 + 3)


def drain(like, sem):
    pltpu.make_async_copy(like, like, sem).wait()


def columns(zz, yy):
    return pl.ds(pl.multiple_of((zz * NY + yy) * HEAD_DIM, HEAD_DIM), HEAD_DIM)


def quarter(yy):
    return pl.ds(pl.multiple_of(yy * ROWS, ROWS), ROWS)


def layer_kernel(rand_hbm, glob_hbm, q_ref, g_ref, k_ref, v_ref, od_out, dkv_out,
                 stage, kv, qg, od, terms, total, table, twin_send, twin, sums, hop, joined, from_left, from_right, final,
                 rand, glob, picks, small_sem, stage_sem, out_sem, ring_out_sem, qg_sem, a_sem, l_sem, r_sem, f_sem, s_sem,
                 twin_out, back_out, od_send, kv_send, twin_sem, hop_sem, bl_sem, br_sem, od_sem, kv_sem):
    z, x, c, y = places()
    zs = [(z + d) % NZ for d in range(NZ)]
    ys = [(y + d) % NY for d in range(NY)]
    right, left, over = (x + 1) % NX, (x + 3) % NX, (x + 2) % NX
    place = x * NC + c
    head = z * NY + y
    loads = [
        pltpu.make_async_copy(src, stage.at[n], stage_sem.at[n])
        for n, src in ((2, k_ref), (3, v_ref), (0, q_ref), (1, g_ref))
    ]
    small = [
        pltpu.make_async_copy(rand_hbm, rand, small_sem.at[0]),
        pltpu.make_async_copy(glob_hbm, glob, small_sem.at[1]),
    ]
    for load in loads + small:
        load.start()
    greet(z, x, c, y, zs, ys)

    def scatter(d, first, dst, sem):
        for n in range(NY):
            part = stage.at[pl.ds(first, 2), :, columns(zs[d], ys[n])]
            if d == 0 and n == 0:
                pltpu.make_async_copy(part, dst, sem).start()
            else:
                pltpu.make_async_remote_copy(
                    src_ref=part, dst_ref=dst, send_sem=out_sem, recv_sem=sem,
                    device_id=(zs[d], x, c, ys[n]), device_id_type=MESH,
                ).start()

    def chunk(zz, xx, cc):
        return kv.at[:, pl.ds(zz * 16 + xx * 4 + cc * 2, 2)]

    loads[0].wait()
    loads[1].wait()
    for d in ORDER:
        scatter(d, 2, kv.at[:, z * 16 + place * 2 + y // 2, quarter(y % 2), :], a_sem.at[z])

    loads[2].wait()
    loads[3].wait()

    picked = pltpu.make_async_copy(table, picks, small_sem.at[0])

    def order_terms():
        small[0].wait()
        small[1].wait()
        lane = lax.broadcasted_iota(jnp.int32, (HEAD_DIM, HEAD_DIM), 1)
        row = lax.broadcasted_iota(jnp.int32, (HEAD_DIM, HEAD_DIM), 0)

        def names(slot):
            out = jnp.where(slot < WINDOW_TERMS, slot // NEAR * 16 + place * 2 - 1 + slot % NEAR, FAR)
            for plane in range(NZ):
                for n in range(2):
                    for r in range(RANDS):
                        at = WINDOW_TERMS + (plane * 2 + n) * RANDS + r
                        out = jnp.where(slot == at, rand[r, head, plane * 16 + place * 2 + n], out)
            for n in range(2):
                out = jnp.where(slot == TERMS - 2 + n, glob[n], out)
            return out

        down = names(row)
        across = jnp.broadcast_to(names(lax.broadcasted_iota(jnp.int32, (1, HEAD_DIM), 1)), (HEAD_DIM, HEAD_DIM))
        ahead = (across < down) | ((across == down) & (lane < row))
        rank = jnp.sum(jnp.where(ahead, 1, 0), axis=1, keepdims=True)
        table[...] = jnp.zeros((8, HEAD_DIM), jnp.int32)
        table[0:1, :] = jnp.sum(jnp.where(rank == lane, row, 0), axis=0, keepdims=True)
        table[1:2, :] = jnp.sum(jnp.where(down < lane, 1, 0), axis=0, keepdims=True)
        table[2:3, :] = jnp.sum(jnp.where(down < lane + 1, 1, 0), axis=0, keepdims=True)
        picked.start()
        terms[TERMS - 2] = jnp.zeros((2, BLOCK, HEAD_DIM), jnp.float32)
        terms[TERMS - 1] = jnp.zeros((2, BLOCK, HEAD_DIM), jnp.float32)

    def send(zz, xx, to, sem):
        pltpu.make_async_remote_copy(
            src_ref=chunk(zz, xx, c), dst_ref=chunk(zz, xx, c), send_sem=ring_out_sem, recv_sem=sem,
            device_id=to, device_id_type=MESH,
        ).start()

    to_right, to_left, to_twin = (z, right, c, y), (z, left, c, y), (z, x, 1 - c, y)
    source = [zs[(NZ - d) % NZ] for d in ORDER]
    for step in range(NZ + LAG2):
        if step == TABLES_AT:
            order_terms()
        if step < NZ:
            zz = source[step]
            drain(chunk(zz, x, c), a_sem.at[zz])
            send(zz, x, to_right, l_sem.at[zz])
            send(zz, x, to_left, r_sem.at[zz])
            send(zz, x, to_twin, s_sem)
            scatter(QORDER[step], 0, qg.at[:, z, quarter(y), :], qg_sem.at[z])
        if LAG1 <= step < NZ + LAG1:
            k = step - LAG1
            zz = source[k]
            drain(chunk(zz, left, c), l_sem.at[zz])
            if k % 2 == 1:
                send(zz, left, to_right, f_sem.at[zz])
            send(zz, left, to_twin, s_sem)
            drain(chunk(zz, right, c), r_sem.at[zz])
            if k % 2 == 0:
                send(zz, right, to_left, f_sem.at[zz])
            send(zz, right, to_twin, s_sem)
        if step >= LAG2:
            zz = source[step - LAG2]
            drain(chunk(zz, over, c), f_sem.at[zz])
            send(zz, over, to_twin, s_sem)
    drain(kv.at[:, pl.ds(0, BLOCKS // 2)], s_sem)

    def give(d, src, dst, send_sem, sem):
        for n in range(NY):
            part = src.at[:, quarter(ys[n]), :]
            if d == 0 and n == 0:
                pltpu.make_async_copy(part, dst.at[:, :, columns(z, y)], sem).start()
            else:
                pltpu.make_async_remote_copy(
                    src_ref=part, dst_ref=dst.at[:, :, columns(z, y)], send_sem=send_sem, recv_sem=sem,
                    device_id=(zs[d], x, c, ys[n]), device_id_type=MESH,
                ).start()

    shared = (NEAR + 2) * BLOCK
    every = shared + RANDS * BLOCK
    pair = 2 * BLOCK
    which = lax.broadcasted_iota(jnp.int32, (pair, every), 1) // BLOCK
    second = lax.broadcasted_iota(jnp.int32, (pair, every), 0) // BLOCK
    planes = [zs[d] for d in BACK]
    for turn in range(NZ // TURN):
        R = range(TURN)
        group = [planes[turn * TURN + n] for n in R]
        q, g, k, v, kr, vr = [], [], [], [], [], []
        for p in group:
            drain(qg.at[:, p], qg_sem.at[p])
            q.append(qg[0, p])
            g.append(qg[1, p])
            first = p * 16 + place * 2
            near = [(first + BLOCKS - 1) % BLOCKS, first, first + 1, (first + 2) % BLOCKS, glob[0], glob[1]]
            far = [[rand[r, head, first + n] for r in range(RANDS)] for n in range(2)]
            k.append(jnp.concatenate([kv[0, b] for b in near], axis=0))
            v.append(jnp.concatenate([kv[1, b] for b in near], axis=0))
            kr.append([jnp.concatenate([kv[0, b] for b in f], axis=0) for f in far])
            vr.append([jnp.concatenate([kv[1, b] for b in f], axis=0) for f in far])

        def halves(a):
            return a[:BLOCK], a[BLOCK:]

        def against(a, b, br):
            alone = jnp.concatenate([dot(h, m, NT) for h, m in zip(halves(a), br)], axis=0)
            return jnp.concatenate([dot(a, b, NT), alone], axis=1)

        def gathered(a, b, br):
            alone = jnp.concatenate([dot(h, m) for h, m in zip(halves(a[:, shared:]), br)], axis=0)
            return dot(a[:, :shared], b) + alone

        s = [against(q[n], k[n], kr[n]) for n in R]
        dp = [against(g[n], v[n], vr[n]) for n in R]
        p_, w, o, ds = [], [], [], []
        for n in R:
            first = group[n] * 16 + place * 2
            gone = (which == 0) & ((second == 1) | (first == 0))
            gone = gone | ((which == 3) & ((second == 0) | (first == BLOCKS - 2)))
            t = jnp.where(gone, -jnp.inf, s[n] * SCALE)
            e = jnp.exp(t - jnp.max(t, axis=1, keepdims=True))
            p_.append(e * (1.0 / jnp.sum(e, axis=1, keepdims=True)))
            w.append(narrow(p_[n]))
        for n in R:
            o.append(narrow(gathered(w[n], v[n], vr[n])))
        for n in R:
            delta = jnp.sum(wide(g[n]) * wide(o[n]), axis=1, keepdims=True)
            ds.append(narrow(p_[n] * (dp[n] - delta)))
        for n in R:
            p = group[n]
            for kind, left_, right_, scale in ((0, ds[n], q[n], SCALE), (1, w[n], g[n], 1.0)):
                both = dot(left_[:, :shared], right_, TN)
                for i in range(NEAR):
                    terms[p * NEAR + i, kind] = scale * both[i * BLOCK:(i + 1) * BLOCK]
                for i in range(2):
                    terms[TERMS - 2 + i, kind] += scale * both[(NEAR + i) * BLOCK:(NEAR + i + 1) * BLOCK]
                for h, (a, b) in enumerate(zip(halves(left_[:, shared:]), halves(right_))):
                    alone = scale * dot(a, b, TN)
                    for r in range(RANDS):
                        at = WINDOW_TERMS + (p * 2 + h) * RANDS + r
                        terms[at, kind] = alone[r * BLOCK:(r + 1) * BLOCK]
        for n in R:
            od[group[n], 0] = o[n]

        def send_rows(turn=turn, group=group, ds=ds, k=k, kr=kr):
            for n in range(TURN):
                od[group[n], 1] = narrow(SCALE * gathered(ds[n], k[n], kr[n]))
                give(BACK[turn * TURN + n], od.at[group[n]], od_out, od_send, od_sem)

        if turn < NZ // TURN - 1:
            send_rows()

    picked.wait()

    total[0] = jnp.zeros((2, BLOCK, HEAD_DIM), jnp.float32)

    def run(n, carry):
        at = picks[0, n]
        carry = (carry[0] + terms[at, 0], carry[1] + terms[at, 1])
        total[n + 1, 0] = carry[0]
        total[n + 1, 1] = carry[1]
        return carry

    nothing = jnp.zeros((BLOCK, HEAD_DIM), jnp.float32)
    lax.fori_loop(0, TERMS, run, (nothing, nothing))

    def partial(kind, zz, xx, cc, half):
        block = zz * 16 + xx * 4 + cc * 2 + half
        return total[picks[2, block], kind] - total[picks[1, block], kind]

    def fill_twin(step):
        def fill(xx, carry):
            for kind in range(2):
                for half in range(2):
                    twin_send[step, kind, xx, half * BLOCK:(half + 1) * BLOCK, :] = narrow(
                        partial(kind, planes[step], xx, 1 - c, half)
                    )
            return carry

        lax.fori_loop(0, NX, fill, 0)
        pltpu.make_async_remote_copy(
            src_ref=twin_send.at[step], dst_ref=twin.at[step], send_sem=twin_out, recv_sem=twin_sem.at[step],
            device_id=to_twin, device_id_type=MESH,
        ).start()

    for step in range(AHEAD):
        fill_twin(step)
    send_rows()

    def pass_on(src, dst, sem, to):
        pltpu.make_async_remote_copy(
            src_ref=src, dst_ref=dst, send_sem=back_out, recv_sem=sem, device_id=to, device_id_type=MESH,
        ).start()

    for step in range(NZ + BACK2):
        if step < NZ - AHEAD:
            fill_twin(step + AHEAD)
        if step < NZ:
            drain(twin.at[step], twin_sem.at[step])

            def add(xx, carry, step=step):
                for kind in range(2):
                    for half in range(2):
                        rows = slice(half * BLOCK, (half + 1) * BLOCK)
                        sums[step, kind, xx, rows, :] = narrow(
                            partial(kind, planes[step], xx, c, half) + wide(twin[step, kind, xx, rows, :])
                        )
                return carry

            lax.fori_loop(0, NX, add, 0)
            if step % 2 == 0:
                pass_on(sums.at[step, :, over], hop.at[step], hop_sem.at[step], to_right)
                pass_on(sums.at[step, :, left], from_right.at[step], br_sem.at[step], to_left)
            else:
                pass_on(sums.at[step, :, over], hop.at[step], hop_sem.at[step], to_left)
                pass_on(sums.at[step, :, right], from_left.at[step], bl_sem.at[step], to_right)
        if BACK1 <= step < NZ + BACK1:
            k = step - BACK1
            drain(hop.at[k], hop_sem.at[k])
            to = right if k % 2 == 0 else left
            for n in range(2):
                joined[k, n] = narrow(wide(sums[k, n, to]) + wide(hop[k, n]))
            if k % 2 == 0:
                pass_on(joined.at[k], from_left.at[k], bl_sem.at[k], to_right)
            else:
                pass_on(joined.at[k], from_right.at[k], br_sem.at[k], to_left)
        if step >= BACK2:
            k = step - BACK2
            drain(from_left.at[k], bl_sem.at[k])
            drain(from_right.at[k], br_sem.at[k])
            for n in range(2):
                final[k, n] = narrow(wide(sums[k, n, x]) + wide(from_left[k, n]) + wide(from_right[k, n]))
            give(BACK[k], final.at[k], dkv_out, kv_send, kv_sem)
    others = pl.ds(0, (NZ * NY - 1) * HEAD_DIM)
    drain(stage.at[:, :, others], out_sem)
    drain(kv.at[:, pl.ds(0, BLOCKS - 16)], ring_out_sem)
    drain(twin_send, twin_out)
    drain(sums.at[:, :, pl.ds(0, NX - 1)], back_out)
    drain(od_out.at[:, :, others], od_send)
    drain(dkv_out.at[:, :, others], kv_send)
    drain(od_out, od_sem)
    drain(dkv_out, kv_sem)


def layer(rand, glob, q, g, k, v):
    dma = pltpu.SemaphoreType.DMA
    hbm = pl.BlockSpec(memory_space=pltpu.HBM)
    anywhere = pl.BlockSpec(memory_space=pl.ANY)
    rows = jax.ShapeDtypeStruct((2, ROWS, WIDTH), jnp.bfloat16)
    half = jnp.bfloat16
    plane = pltpu.VMEM((NZ, 2, NY * ROWS, HEAD_DIM), half)
    planes = pltpu.VMEM((NZ, 2, NX, NY * ROWS, HEAD_DIM), half)
    each = dma((NZ,))
    return pl.pallas_call(
        layer_kernel,
        out_shape=(rows, rows),
        in_specs=[hbm] * 6,
        out_specs=(anywhere, anywhere),
        scratch_shapes=[
            pltpu.VMEM((4, ROWS, WIDTH), half),
            pltpu.VMEM((2, BLOCKS, BLOCK, HEAD_DIM), half),
            pltpu.VMEM((2, NZ, NY * ROWS, HEAD_DIM), half),
            plane,
            pltpu.VMEM((TERMS, 2, BLOCK, HEAD_DIM), jnp.float32),
            pltpu.VMEM((TERMS + 1, 2, BLOCK, HEAD_DIM), jnp.float32),
            pltpu.VMEM((8, HEAD_DIM), jnp.int32),
            planes, planes, planes, plane, plane, plane, plane, plane,
            pltpu.SMEM(rand.shape, jnp.int32),
            pltpu.SMEM(glob.shape, jnp.int32),
            pltpu.SMEM((8, HEAD_DIM), jnp.int32),
            dma((2,)), dma((4,)), dma, dma, each, each, each, each, each, dma,
            dma, dma, dma, dma, each, each, each, each, dma, dma,
        ],
        compiler_params=pltpu.CompilerParams(
            collective_id=0, has_side_effects=True, vmem_limit_bytes=48 * 1024 * 1024
        ),
    )(*(pltpu.with_memory_space_constraint(a, pltpu.HBM) for a in (rand, glob, q, g, k, v)))


def body(queries, keys, values, grad_out, random_blocks, global_blocks):
    rand = jnp.transpose(random_blocks, (2, 0, 1))
    od, dkv = layer(rand, global_blocks, queries, grad_out, keys, values)
    return od[0], od[1], dkv[0], dkv[1]


def solution(mesh):
    fine = jax.sharding.Mesh(mesh.devices.reshape(NZ, NX, NC, NY), ("z", "x", "core", "head"))
    rows = P(("z", "x", "core", "head"), None)
    return jax.shard_map(
        body,
        mesh=fine,
        in_specs=(rows, rows, rows, rows, P(), P()),
        out_specs=(rows, rows, rows, rows),
        check_vma=False,
    )
```
